256 devices in a mesh: prompt: 4 (over y), rollout: 8 (over z), head: 8 (over x, core).
Axes of the slice: x: 4, y: 4, z: 8, core: 2. Of those that a mesh axis runs over, the one named last changes fastest.
Arguments:
- queries: bfloat16 [32, 512, 8, 384], P(('prompt', 'rollout'), None, 'head'), parts along dimension 0
- own_keys: bfloat16 [32, 512, 8, 128], P(('prompt', 'rollout'), None, 'head'), parts along dimension 0, may hold values from -6 to 6
- own_values: bfloat16 [32, 512, 8, 128], P(('prompt', 'rollout'), None, 'head'), parts along dimension 0, may hold values from -6 to 6
- grad_out: bfloat16 [32, 512, 8, 384], P(('prompt', 'rollout'), None, 'head'), parts along dimension 0, may hold values from -6 to 6
- prefix_kv: bfloat16 [2, 4096, 1024], P(None, ('prompt', 'rollout', 'head')), parts along dimension 1
- lengths: int32 [32], P(('prompt', 'rollout')), parts along dimension 0, may hold values from 128 to 512, as said below
Outputs:
- grad_queries: bfloat16 [32, 512, 8, 384], P(('prompt', 'rollout'), None, 'head'), parts along dimension 0
- grad_own: bfloat16 [2, 32, 512, 8, 128], P(None, ('prompt', 'rollout'), None, 'head'), parts along dimension 1
- grad_prefix: bfloat16 [2, 4096, 1024], P(None, ('prompt', 'rollout', 'head')), parts along dimension 1
The draws below stay inside these ranges and needn't reach their ends.
There are 4 independent parts, one for each index of `prompt`. The reference program is written for one: setup_inputs(seed, part) draws one part's arguments, and reference() takes and returns one part's arrays. A program takes and returns all parts, laid end to end along the dimension named above; each array names one. Nothing has to cross between parts.
Inputs may be any that keep to these rules, and one draw needn't show every extreme that they name: `lengths`: every rollout has at least 128 tokens, and some rollout of each prompt fills all 512 slots.
All inputs are finite; a program needn't handle non-finite values.
Results may differ from the reference program's by a relative error of at most 0.019.
Values may be sent and summed in bfloat16 or wider, within the bound.
No kernel may reach another device: no remote copies, remote signals or barrier semaphores. Data moves between devices by JAX's collectives and lax.ppermute only.
A program may use at most 64 MiB of HBM per device.

```python
import math
import jax
import jax.numpy as jnp
from jax import lax

HD = 128
QH = 3
MAXLEN = 512
PREFIX = 1024
KVH = 8
ROLLOUTS = 8


def shared_prefix(key, closeness):
    base = jax.random.normal(jax.random.fold_in(key, 11), (2, PREFIX, KVH, HD), jnp.float32)
    picks = jax.random.randint(jax.random.fold_in(key, 12), (ROLLOUTS, 4, KVH), 0, PREFIX - 1)
    keys_base = base[0]
    targets = (picks + 1).transpose(2, 0, 1).reshape(KVH, ROLLOUTS * 4)
    marked = jnp.any(jnp.arange(PREFIX)[:, None, None] == targets[None, :, :], axis=2).astype(jnp.float32)
    weight_near = closeness * marked[:, :, None]
    keys_new = keys_base * (1.0 - weight_near)
    return jnp.stack([keys_new, base[1]])


def draw_prefix_kv(key, part):
    prefix = shared_prefix(key, 0.0)
    return prefix.reshape(2, PREFIX, KVH * HD).astype(jnp.bfloat16)


def draw_queries(key, part):
    key = jax.random.fold_in(key, 5)
    values = jax.random.normal(key, (ROLLOUTS, MAXLEN, KVH, QH * HD), jnp.float32)
    return values.astype(jnp.bfloat16)


def draw_lengths(key, part):
    key = jax.random.fold_in(key, 7)
    drawn = jax.random.randint(key, (ROLLOUTS,), MAXLEN // 4, MAXLEN + 1)
    chosen = jax.random.randint(jax.random.fold_in(key, 8), (), 0, ROLLOUTS)
    return jnp.where(jnp.arange(ROLLOUTS) == chosen, MAXLEN, drawn).astype(jnp.int32)


def levels(stream_key, shape, cuts, low, high):
    level, own = 1.0, jax.random.fold_in(stream_key, 6)
    for position, parts in cuts:
        draws = jnp.exp(jax.random.uniform(jax.random.fold_in(own, position), (parts,), jnp.float32, low / len(cuts), high / len(cuts)))
        level = level * jnp.repeat(draws, shape[position] // parts).reshape([-1 if axis == position else 1 for axis in range(len(shape))])
    return level


def noise(key, extent, width, limit, cuts=(), kind=jnp.bfloat16):
    gain = levels(key, extent, cuts, -0.22, 0.18) if cuts else 1.0
    array = jax.random.normal(key, extent, jnp.float32) * width * gain
    return jnp.minimum(jnp.maximum(array, -limit), limit).astype(kind)


def setup_inputs(seed: int = 0, part: int = 0) -> dict:
    keys = jax.random.split(jax.random.key(seed), 7)
    part_keys = jax.random.split(jax.random.fold_in(keys[6], part), 7)
    queries = draw_queries(jax.random.fold_in(jax.random.fold_in(keys[6], part), 71), part)
    own_keys = noise(part_keys[1], (ROLLOUTS, MAXLEN, KVH, HD), 1.0, 6.0, ((0, 8), (2, 8)))
    own_values = noise(part_keys[2], (ROLLOUTS, MAXLEN, KVH, HD), 1.0, 6.0, ((0, 8), (2, 8)))
    grad_out = noise(part_keys[3], (ROLLOUTS, MAXLEN, KVH, QH * HD), 1.0, 6.0, ((0, 8), (2, 8)))
    prefix_kv = draw_prefix_kv(jax.random.fold_in(jax.random.fold_in(keys[6], part), 71), part)
    lengths = draw_lengths(jax.random.fold_in(jax.random.fold_in(keys[6], part), 71), part)
    return dict(queries=queries, own_keys=own_keys, own_values=own_values, grad_out=grad_out, prefix_kv=prefix_kv, lengths=lengths)


def attend_grads(query_rows, grad_rows, keys_all, values_all, allowed, scaling):
    scores = jnp.einsum('hid,jd->hij', query_rows, keys_all) * scaling
    scores = jnp.where(allowed[None], scores, -1e+30)
    row_max = lax.optimization_barrier(jnp.max(scores, axis=2, keepdims=True))
    raised = jnp.exp(scores - row_max)
    weights = raised / lax.optimization_barrier(jnp.sum(raised, axis=2, keepdims=True))
    grad_weights = jnp.einsum('hid,jd->hij', grad_rows, values_all)
    row_dot = lax.optimization_barrier(jnp.sum(weights * grad_weights, axis=2, keepdims=True))
    weights_low = lax.optimization_barrier(weights.astype(jnp.bfloat16)).astype(jnp.float32)
    grad_scores = lax.optimization_barrier((weights * (grad_weights - row_dot)).astype(jnp.bfloat16)).astype(jnp.float32)
    grad_query = jnp.einsum('hij,jd->hid', grad_scores, keys_all) * scaling
    grad_keys = jnp.einsum('hij,hid->jd', grad_scores, query_rows) * scaling
    grad_values = jnp.einsum('hij,hid->jd', weights_low, grad_rows)
    return (grad_query, grad_keys, grad_values)

def reference(queries, own_keys, own_values, grad_out, prefix_kv, lengths):
    rollout_count = queries.shape[0]
    scaling = 1.0 / math.sqrt(HD)
    prefix = prefix_kv.reshape(2, PREFIX, KVH, HD)
    positions = jnp.arange(MAXLEN, dtype=jnp.int32)
    columns = jnp.arange(PREFIX + MAXLEN, dtype=jnp.int32)
    allowed = (columns[None, :] < PREFIX) | (columns[None, :] - PREFIX <= positions[:, None])

    def one_item(item_index):
        rollout = item_index // KVH
        kv_group = item_index % KVH
        query_rows = queries[rollout, :, kv_group].reshape(MAXLEN, QH, HD).astype(jnp.float32).transpose(1, 0, 2)
        live_rows = (positions < lengths[rollout]).astype(jnp.float32)
        grad_rows = grad_out[rollout, :, kv_group].reshape(MAXLEN, QH, HD).astype(jnp.float32)
        grad_rows = (grad_rows * live_rows[:, None, None]).transpose(1, 0, 2)
        keys_all = jnp.concatenate([prefix[0, :, kv_group], own_keys[rollout, :, kv_group]], 0).astype(jnp.float32)
        values_all = jnp.concatenate([prefix[1, :, kv_group], own_values[rollout, :, kv_group]], 0).astype(jnp.float32)
        grad_query, grad_keys, grad_values = attend_grads(query_rows, grad_rows, keys_all, values_all, allowed, scaling)
        grad_query = grad_query.transpose(1, 0, 2).reshape(MAXLEN, QH * HD).astype(jnp.bfloat16)
        return (grad_query, grad_keys, grad_values)
    items = jnp.arange(rollout_count * KVH, dtype=jnp.int32)
    grad_query, grad_keys, grad_values = lax.map(one_item, items)
    grad_queries = grad_query.reshape(rollout_count, KVH, MAXLEN, QH * HD).transpose(0, 2, 1, 3)
    grad_keys = grad_keys.reshape(rollout_count, KVH, PREFIX + MAXLEN, HD)
    grad_values = grad_values.reshape(rollout_count, KVH, PREFIX + MAXLEN, HD)
    grad_own = jnp.stack([grad_keys[:, :, PREFIX:], grad_values[:, :, PREFIX:]]).transpose(0, 1, 3, 2, 4).astype(jnp.bfloat16)
    prefix_keys = lax.optimization_barrier(jnp.sum(grad_keys[:, :, :PREFIX], axis=0)).transpose(1, 0, 2).reshape(PREFIX, KVH * HD)
    prefix_values = lax.optimization_barrier(jnp.sum(grad_values[:, :, :PREFIX], axis=0)).transpose(1, 0, 2).reshape(PREFIX, KVH * HD)
    grad_prefix = jnp.stack([prefix_keys, prefix_values]).astype(jnp.bfloat16)
    return (grad_queries, grad_own, grad_prefix)
```

```python
import functools
import math

import jax
import jax.numpy as jnp
from jax import lax
from jax.experimental import pallas as pl
from jax.experimental.pallas import tpu as pltpu
from jax.sharding import PartitionSpec as P

F32 = jnp.float32
BF16 = jnp.bfloat16
NEG = -1e30
LOG2E = math.log2(math.e)
VMEM_BYTES = 56 * 1024 * 1024


def dot_last(a, b):
    return lax.dot_general(a, b, (((1,), (1,)), ((), ())), preferred_element_type=F32)


def dot_plain(a, b):
    return lax.dot_general(a, b, (((1,), (0,)), ((), ())), preferred_element_type=F32)


def fold(x, op):
    parts = [x[i : i + 8] for i in range(0, x.shape[0], 8)]
    while len(parts) > 1:
        parts = [
            op(parts[i], parts[i + 1]) if i + 1 < len(parts) else parts[i]
            for i in range(0, len(parts), 2)
        ]
    return parts[0]


def live_grad(grad_ref, length, head, hd):
    g = grad_ref[:, head * hd : (head + 1) * hd]
    rows = lax.broadcasted_iota(jnp.int32, g.shape, 0)
    return jnp.where(rows < length, g, jnp.zeros_like(g))


def causal(rows_of_keys, first_key, columns, first_column):
    key = lax.broadcasted_iota(jnp.int32, (rows_of_keys, columns), 0) + first_key
    row = lax.broadcasted_iota(jnp.int32, (rows_of_keys, columns), 1) + first_column
    return key <= row


def own_stats_kernel(len_ref, q_ref, g_ref, k_ref, v_ref, m_ref, l_ref, d_ref, *, heads, hd, c):
    n = q_ref.shape[0]
    half = n // 2
    length = len_ref[0]
    for h in range(heads):
        q = q_ref[:, h * hd : (h + 1) * hd]
        g = live_grad(g_ref, length, h, hd)
        for b in range(2):
            cols = slice(b * half, (b + 1) * half)
            keys = (b + 1) * half
            s = dot_last(k_ref[0:keys], q[cols]) * c
            s = jnp.where(causal(keys, 0, half, b * half), s, NEG)
            m = jnp.max(fold(s, jnp.maximum), axis=0, keepdims=True)
            p = jnp.exp2(s - m)
            dp = dot_last(v_ref[0:keys], g[cols])
            m_ref[h : h + 1, cols] = m
            l_ref[h : h + 1, cols] = jnp.sum(fold(p, jnp.add), axis=0, keepdims=True)
            d_ref[h : h + 1, cols] = jnp.sum(fold(p * dp, jnp.add), axis=0, keepdims=True)


def prefix_kernel(
    len_ref, q_ref, g_ref, kv_ref, m_ref, l_ref, d_ref,
    send_ref, shift_ref, dot_ref,
    qs_ref, gs_ref, s_ref, dp_ref, w_ref, ds_ref,
    *, heads, hd, c, scaling
):
    n = q_ref.shape[0]
    devices, _, rows, _ = kv_ref.shape
    prefix = devices * rows
    step = 256
    per = step // rows
    length = len_ref[0]
    for h in range(heads):
        qs_ref[h * n : (h + 1) * n] = q_ref[:, h * hd : (h + 1) * hd]
        gs_ref[h * n : (h + 1) * n] = live_grad(g_ref, length, h, hd)
    chunks = prefix // step
    for h in range(heads):
        q = qs_ref[h * n : (h + 1) * n]
        g = gs_ref[h * n : (h + 1) * n]
        top = None
        for i in range(chunks):
            k = kv_ref[i * per : (i + 1) * per, 0].reshape(step, hd)
            s = dot_last(k, q) * c
            s_ref[i * step : (i + 1) * step] = s
            f = fold(s, jnp.maximum)
            top = f if top is None else jnp.maximum(top, f)
        m_own = m_ref[h : h + 1]
        m = jnp.maximum(m_own, jnp.max(top, axis=0, keepdims=True))
        l8, d8 = None, None
        for i in range(chunks):
            v = kv_ref[i * per : (i + 1) * per, 1].reshape(step, hd)
            dp = dot_last(v, g)
            dp_ref[i * step : (i + 1) * step] = dp
            p = jnp.exp2(s_ref[i * step : (i + 1) * step] - m)
            s_ref[i * step : (i + 1) * step] = p
            fl = fold(p, jnp.add)
            fd = fold(p * dp, jnp.add)
            l8 = fl if l8 is None else l8 + fl
            d8 = fd if d8 is None else d8 + fd
        again = jnp.exp2(m_own - m)
        l = l_ref[h : h + 1] * again + jnp.sum(l8, axis=0, keepdims=True)
        d = d_ref[h : h + 1] * again + jnp.sum(d8, axis=0, keepdims=True)
        inv = 1.0 / l
        d = d * inv
        shift_ref[h : h + 1] = m + jnp.log2(l)
        dot_ref[h : h + 1] = d
        for i in range(chunks):
            part = slice(i * step, (i + 1) * step)
            w = s_ref[part] * inv
            w_ref[part, h * n : (h + 1) * n] = w.astype(BF16)
            ds_ref[part, h * n : (h + 1) * n] = (w * (dp_ref[part] - d)).astype(BF16)
    for i in range(chunks):
        part = slice(i * step, (i + 1) * step)
        grad_k = dot_plain(ds_ref[part], qs_ref[...]) * scaling
        grad_v = dot_plain(w_ref[part], gs_ref[...])
        send_ref[i * per : (i + 1) * per, 0] = grad_k.astype(BF16).reshape(per, rows, hd)
        send_ref[i * per : (i + 1) * per, 1] = grad_v.astype(BF16).reshape(per, rows, hd)


def rest_kernel(
    len_ref, q_ref, g_ref, kv_ref, k_ref, v_ref, shift_ref, dot_ref,
    dq_ref, own_ref,
    qs_ref, gs_ref, kt_ref, w_ref, ds_ref,
    *, heads, hd, c, scaling
):
    n = q_ref.shape[0]
    devices, _, rows, _ = kv_ref.shape
    prefix = devices * rows
    step = 256
    per = step // rows
    half = n // 2
    length = len_ref[0]
    chunks = prefix // step
    for h in range(heads):
        qs_ref[h * n : (h + 1) * n] = q_ref[:, h * hd : (h + 1) * hd]
        gs_ref[h * n : (h + 1) * n] = live_grad(g_ref, length, h, hd)
    for i in range(chunks):
        k = kv_ref[i * per : (i + 1) * per, 0].reshape(step, hd)
        kt_ref[:, i * step : (i + 1) * step] = k.T
    kt_ref[:, prefix:] = k_ref[...].T
    for h in range(heads):
        shift = shift_ref[h : h + 1]
        d = dot_ref[h : h + 1]
        q = qs_ref[h * n : (h + 1) * n]
        g = gs_ref[h * n : (h + 1) * n]
        for i in range(chunks):
            k = kv_ref[i * per : (i + 1) * per, 0].reshape(step, hd)
            v = kv_ref[i * per : (i + 1) * per, 1].reshape(step, hd)
            w = jnp.exp2(dot_last(k, q) * c - shift)
            ds_ref[i * step : (i + 1) * step] = (w * (dot_last(v, g) - d)).astype(BF16)
        for b in range(2):
            cols = slice(b * half, (b + 1) * half)
            keys = (b + 1) * half
            s = dot_last(k_ref[0:keys], q[cols]) * c
            s = jnp.where(causal(keys, 0, half, b * half), s, NEG)
            w = jnp.exp2(s - shift[:, cols])
            ds = (w * (dot_last(v_ref[0:keys], g[cols]) - d[:, cols])).astype(BF16)
            at = slice(h * n + b * half, h * n + (b + 1) * half)
            w_ref[0:keys, at] = w.astype(BF16)
            ds_ref[prefix : prefix + keys, cols] = ds
            if keys < n:
                empty = jnp.zeros((n - keys, half), BF16)
                w_ref[keys:, at] = empty
                ds_ref[prefix + keys :, cols] = empty
        dqt = dot_plain(kt_ref[...], ds_ref[...]) * scaling
        dq_ref[:, h * hd : (h + 1) * hd] = dqt.T.astype(BF16)
        own = dot_plain(ds_ref[prefix:], q)
        total = own if h == 0 else total + own
    own_ref[0] = (total * scaling).astype(BF16)
    own_ref[1] = dot_plain(w_ref[...], gs_ref[...]).astype(BF16)


def sum_kernel(x_ref, out_ref):
    groups, heads, _, rows, hd = x_ref.shape
    for h in range(heads):
        total = x_ref[0, h].astype(F32)
        for r in range(1, groups):
            total = total + x_ref[r, h].astype(F32)
        out_ref[:, :, h * hd : (h + 1) * hd] = total.astype(BF16)


def per_device(queries, own_keys, own_values, grad_out, prefix_kv, lengths):
    hd = own_keys.shape[3]
    n = queries.shape[1]
    heads = queries.shape[3] // hd
    rollouts = lax.axis_size("rollout")
    head_devices = lax.axis_size("head")
    devices = rollouts * head_devices
    rows = prefix_kv.shape[1]
    prefix = devices * rows
    scaling = 1.0 / math.sqrt(hd)
    c = scaling * LOG2E
    q = queries.reshape(n, heads * hd)
    g = grad_out.reshape(n, heads * hd)
    k_own = own_keys.reshape(n, hd)
    v_own = own_values.reshape(n, hd)

    smem = pl.BlockSpec(memory_space=pltpu.SMEM)
    vmem = pl.BlockSpec(memory_space=pltpu.VMEM)
    params = pltpu.CompilerParams(vmem_limit_bytes=VMEM_BYTES)
    stat = jax.ShapeDtypeStruct((heads, n), F32)

    by_head = prefix_kv.reshape(2, rows, head_devices, hd).transpose(2, 0, 1, 3)
    outgoing = jnp.broadcast_to(by_head[None], (rollouts,) + by_head.shape)
    outgoing = outgoing.reshape(devices, 2, rows, hd)
    kv = lax.all_to_all(outgoing, ("rollout", "head"), 0, 0, tiled=True)

    m_own, l_own, d_own = pl.pallas_call(
        functools.partial(own_stats_kernel, heads=heads, hd=hd, c=c),
        out_shape=(stat, stat, stat),
        in_specs=[smem, vmem, vmem, vmem, vmem],
        out_specs=(vmem, vmem, vmem),
        compiler_params=params,
        cost_estimate=pl.CostEstimate(
            flops=4 * heads * n * n * hd, bytes_accessed=3 << 20, transcendentals=heads * n * n
        ),
        name="own_stats",
    )(lengths, q, g, k_own, v_own)

    grads, shift, row_dot = pl.pallas_call(
        functools.partial(prefix_kernel, heads=heads, hd=hd, c=c, scaling=scaling),
        out_shape=(jax.ShapeDtypeStruct((devices, 2, rows, hd), BF16), stat, stat),
        in_specs=[smem] + [vmem] * 6,
        out_specs=(vmem, vmem, vmem),
        scratch_shapes=[
            pltpu.VMEM((heads * n, hd), BF16),
            pltpu.VMEM((heads * n, hd), BF16),
            pltpu.VMEM((prefix, n), F32),
            pltpu.VMEM((prefix, n), F32),
            pltpu.VMEM((prefix, heads * n), BF16),
            pltpu.VMEM((prefix, heads * n), BF16),
        ],
        compiler_params=params,
        cost_estimate=pl.CostEstimate(
            flops=8 * heads * n * prefix * hd, bytes_accessed=3 << 20, transcendentals=heads * n * prefix
        ),
        name="prefix_grads",
    )(lengths, q, g, kv, m_own, l_own, d_own)

    parts = lax.all_to_all(grads, ("rollout", "head"), 0, 0, tiled=True)

    dq, own = pl.pallas_call(
        functools.partial(rest_kernel, heads=heads, hd=hd, c=c, scaling=scaling),
        out_shape=(
            jax.ShapeDtypeStruct((n, heads * hd), BF16),
            jax.ShapeDtypeStruct((2, n, hd), BF16),
        ),
        in_specs=[smem] + [vmem] * 7,
        out_specs=(vmem, vmem),
        scratch_shapes=[
            pltpu.VMEM((heads * n, hd), BF16),
            pltpu.VMEM((heads * n, hd), BF16),
            pltpu.VMEM((hd, prefix + n), BF16),
            pltpu.VMEM((n, heads * n), BF16),
            pltpu.VMEM((prefix + n, n), BF16),
        ],
        compiler_params=params,
        cost_estimate=pl.CostEstimate(
            flops=8 * heads * n * (prefix + n) * hd,
            bytes_accessed=4 << 20,
            transcendentals=heads * n * (prefix + n),
        ),
        name="query_and_own_grads",
    )(lengths, q, g, kv, k_own, v_own, shift, row_dot)

    grad_prefix = pl.pallas_call(
        sum_kernel,
        out_shape=jax.ShapeDtypeStruct((2, rows, head_devices * hd), BF16),
        in_specs=[vmem],
        out_specs=vmem,
        compiler_params=params,
        name="sum_rollouts",
    )(parts.reshape(rollouts, head_devices, 2, rows, hd))

    return (
        dq.reshape(1, n, 1, heads * hd),
        own.reshape(2, 1, n, 1, hd),
        grad_prefix,
    )


def solution(mesh):
    placed = (
        P(("prompt", "rollout"), None, "head", None),
        P(("prompt", "rollout"), None, "head", None),
        P(("prompt", "rollout"), None, "head", None),
        P(("prompt", "rollout"), None, "head", None),
        P(None, ("prompt", "rollout", "head"), None),
        P(("prompt", "rollout")),
    )
    return jax.shard_map(
        per_device,
        mesh=mesh,
        in_specs=placed,
        out_specs=(
            P(("prompt", "rollout"), None, "head", None),
            P(None, ("prompt", "rollout"), None, "head", None),
            P(None, ("prompt", "rollout", "head"), None),
        ),
        check_vma=False,
    )
```

```python
import functools
import math

import jax
import jax.numpy as jnp
from jax import lax
from jax.experimental import pallas as pl
from jax.experimental.pallas import tpu as pltpu
from jax.sharding import PartitionSpec as P

F32 = jnp.float32
BF16 = jnp.bfloat16
NEG = -1e30
LOG2E = math.log2(math.e)
MIB = 1024 * 1024


def dot_last(a, b):
    return lax.dot_general(a, b, (((1,), (1,)), ((), ())), preferred_element_type=F32)


def dot_plain(a, b):
    return lax.dot_general(a, b, (((1,), (0,)), ((), ())), preferred_element_type=F32)


def fold(x, op):
    parts = [x[i : i + 8] for i in range(0, x.shape[0], 8)]
    while len(parts) > 1:
        parts = [
            op(parts[i], parts[i + 1]) if i + 1 < len(parts) else parts[i]
            for i in range(0, len(parts), 2)
        ]
    return parts[0]


def live_grad(grad_ref, length, head, hd):
    g = grad_ref[:, head * hd : (head + 1) * hd]
    rows = lax.broadcasted_iota(jnp.int32, g.shape, 0)
    return jnp.where(rows < length, g, jnp.zeros_like(g))


def causal(rows_of_keys, first_key, columns, first_column):
    key = lax.broadcasted_iota(jnp.int32, (rows_of_keys, columns), 0) + first_key
    row = lax.broadcasted_iota(jnp.int32, (rows_of_keys, columns), 1) + first_column
    return key <= row


def own_stats_kernel(len_ref, q_ref, g_ref, k_ref, v_ref, m_ref, l_ref, d_ref, *, heads, hd, c):
    n = q_ref.shape[0]
    half = n // 2
    length = len_ref[0]
    for h in range(heads):
        q = q_ref[:, h * hd : (h + 1) * hd]
        g = live_grad(g_ref, length, h, hd)
        for b in range(2):
            cols = slice(b * half, (b + 1) * half)
            keys = (b + 1) * half
            s = dot_last(k_ref[0:keys], q[cols]) * c
            s = jnp.where(causal(keys, 0, half, b * half), s, NEG)
            m = jnp.max(fold(s, jnp.maximum), axis=0, keepdims=True)
            p = jnp.exp2(s - m)
            dp = dot_last(v_ref[0:keys], g[cols])
            m_ref[h : h + 1, cols] = m
            l_ref[h : h + 1, cols] = jnp.sum(fold(p, jnp.add), axis=0, keepdims=True)
            d_ref[h : h + 1, cols] = jnp.sum(fold(p * dp, jnp.add), axis=0, keepdims=True)


def prefix_kernel(
    len_ref, q_ref, g_ref, kv_ref, m_ref, l_ref, d_ref,
    send_ref, shift_ref, dot_ref,
    qs_ref, gs_ref, p_ref, dp_ref, w_ref, ds_ref,
    *, heads, hd, c, scaling
):
    n = q_ref.shape[0]
    devices, _, rows, _ = kv_ref.shape
    prefix = devices * rows
    step, width, last = 128, 256, 256
    per = step // rows
    length = len_ref[0]
    for h in range(heads):
        qs_ref[h * n : (h + 1) * n] = q_ref[:, h * hd : (h + 1) * hd]
        gs_ref[h * n : (h + 1) * n] = live_grad(g_ref, length, h, hd)
    chunks = prefix // step

    def block(index, which):
        return kv_ref[index * per : (index + 1) * per, which].reshape(step, hd)

    def spread(x):
        return jnp.broadcast_to(x[None], (step // 8, 8, width)).reshape(step, width)

    for h in range(heads):
        for b in range(n // width):
            cols = slice(b * width, (b + 1) * width)
            at = slice(h * n + b * width, h * n + (b + 1) * width)
            q = qs_ref[at]
            g = gs_ref[at]
            m_own = m_ref[h : h + 1, cols]
            m8 = jnp.broadcast_to(m_own, (8, width))
            l8 = jnp.zeros((8, width), F32)
            d8 = jnp.zeros((8, width), F32)
            tops = []
            for i in range(chunks):
                part = slice(i * step, (i + 1) * step)
                s = dot_last(block(i, 0), q) * c
                top = jnp.maximum(m8, fold(s, jnp.maximum))
                p = jnp.exp2(s - spread(top))
                dp = dot_last(block(i, 1), g)
                again = jnp.exp2(m8 - top)
                l8 = l8 * again + fold(p, jnp.add)
                d8 = d8 * again + fold(p * dp, jnp.add)
                m8 = top
                tops.append(top)
                p_ref[part, cols] = p
                dp_ref[part, cols] = dp
            m = jnp.max(m8, axis=0, keepdims=True)
            again = jnp.exp2(m8 - m)
            again_own = jnp.exp2(m_own - m)
            l = l_ref[h : h + 1, cols] * again_own + jnp.sum(l8 * again, axis=0, keepdims=True)
            d = d_ref[h : h + 1, cols] * again_own + jnp.sum(d8 * again, axis=0, keepdims=True)
            d = d / l
            shift = m + jnp.log2(l)
            shift_ref[h : h + 1, cols] = shift
            dot_ref[h : h + 1, cols] = d
            for i in range(chunks):
                part = slice(i * step, (i + 1) * step)
                w = p_ref[part, cols] * spread(jnp.exp2(tops[i] - shift))
                w_ref[part, at] = w.astype(BF16)
                ds_ref[part, at] = (w * (dp_ref[part, cols] - d)).astype(BF16)
    per = last // rows
    for i in range(prefix // last):
        part = slice(i * last, (i + 1) * last)
        grad_k = dot_plain(ds_ref[part], qs_ref[...]) * scaling
        grad_v = dot_plain(w_ref[part], gs_ref[...])
        send_ref[i * per : (i + 1) * per, 0] = grad_k.astype(BF16).reshape(per, rows, hd)
        send_ref[i * per : (i + 1) * per, 1] = grad_v.astype(BF16).reshape(per, rows, hd)


def rest_kernel(
    len_ref, q_ref, g_ref, kv_ref, k_ref, v_ref, shift_ref, dot_ref,
    dq_ref, own_ref,
    qs_ref, gs_ref, kt_ref, w_ref, ds_ref,
    *, heads, hd, c, scaling
):
    n = q_ref.shape[0]
    devices, _, rows, _ = kv_ref.shape
    prefix = devices * rows
    step = 256
    per = step // rows
    half = n // 2
    length = len_ref[0]
    chunks = prefix // step
    for h in range(heads):
        qs_ref[h * n : (h + 1) * n] = q_ref[:, h * hd : (h + 1) * hd]
        gs_ref[h * n : (h + 1) * n] = live_grad(g_ref, length, h, hd)
    for i in range(chunks):
        k = kv_ref[i * per : (i + 1) * per, 0].reshape(step, hd)
        kt_ref[:, i * step : (i + 1) * step] = k.T
    kt_ref[:, prefix:] = k_ref[...].T
    for h in range(heads):
        shift = shift_ref[h : h + 1]
        d = dot_ref[h : h + 1]
        q = qs_ref[h * n : (h + 1) * n]
        g = gs_ref[h * n : (h + 1) * n]
        for i in range(chunks):
            k = kv_ref[i * per : (i + 1) * per, 0].reshape(step, hd)
            v = kv_ref[i * per : (i + 1) * per, 1].reshape(step, hd)
            w = jnp.exp2(dot_last(k, q) * c - shift)
            ds_ref[i * step : (i + 1) * step] = (w * (dot_last(v, g) - d)).astype(BF16)
        for b in range(2):
            cols = slice(b * half, (b + 1) * half)
            keys = (b + 1) * half
            s = dot_last(k_ref[0:keys], q[cols]) * c
            s = jnp.where(causal(keys, 0, half, b * half), s, NEG)
            w = jnp.exp2(s - shift[:, cols])
            ds = (w * (dot_last(v_ref[0:keys], g[cols]) - d[:, cols])).astype(BF16)
            at = slice(h * n + b * half, h * n + (b + 1) * half)
            w_ref[0:keys, at] = w.astype(BF16)
            ds_ref[prefix : prefix + keys, cols] = ds
            if keys < n:
                empty = jnp.zeros((n - keys, half), BF16)
                w_ref[keys:, at] = empty
                ds_ref[prefix + keys :, cols] = empty
        dqt = dot_plain(kt_ref[...], ds_ref[...]) * scaling
        dq_ref[:, h * hd : (h + 1) * hd] = dqt.T.astype(BF16)
        own = dot_plain(ds_ref[prefix:], q)
        total = own if h == 0 else total + own
    own_ref[0] = (total * scaling).astype(BF16)
    own_ref[1] = dot_plain(w_ref[...], gs_ref[...]).astype(BF16)


def sum_kernel(x_ref, out_ref):
    groups, heads, _, rows, hd = x_ref.shape
    for h in range(heads):
        total = x_ref[0, h].astype(F32)
        for r in range(1, groups):
            total = total + x_ref[r, h].astype(F32)
        out_ref[:, :, h * hd : (h + 1) * hd] = total.astype(BF16)


def per_device(queries, own_keys, own_values, grad_out, prefix_kv, lengths):
    hd = own_keys.shape[3]
    n = queries.shape[1]
    heads = queries.shape[3] // hd
    rollouts = lax.axis_size("rollout")
    head_devices = lax.axis_size("head")
    devices = rollouts * head_devices
    rows = prefix_kv.shape[1]
    prefix = devices * rows
    scaling = 1.0 / math.sqrt(hd)
    c = scaling * LOG2E
    q = queries.reshape(n, heads * hd)
    g = grad_out.reshape(n, heads * hd)
    k_own = own_keys.reshape(n, hd)
    v_own = own_values.reshape(n, hd)

    smem = pl.BlockSpec(memory_space=pltpu.SMEM)
    vmem = pl.BlockSpec(memory_space=pltpu.VMEM)
    stat = jax.ShapeDtypeStruct((heads, n), F32)

    by_head = prefix_kv.reshape(2, rows, head_devices, hd).transpose(2, 0, 1, 3)
    outgoing = jnp.broadcast_to(by_head[None], (rollouts,) + by_head.shape)
    outgoing = outgoing.reshape(devices, 2, rows, hd)
    kv = lax.all_to_all(outgoing, ("rollout", "head"), 0, 0, tiled=True)

    m_own, l_own, d_own = pl.pallas_call(
        functools.partial(own_stats_kernel, heads=heads, hd=hd, c=c),
        out_shape=(stat, stat, stat),
        in_specs=[smem, vmem, vmem, vmem, vmem],
        out_specs=(vmem, vmem, vmem),
        compiler_params=pltpu.CompilerParams(vmem_limit_bytes=12 * MIB),
        cost_estimate=pl.CostEstimate(
            flops=4 * heads * n * n * hd, bytes_accessed=3 << 20, transcendentals=heads * n * n
        ),
        name="own_stats",
    )(lengths, q, g, k_own, v_own)

    grads, shift, row_dot = pl.pallas_call(
        functools.partial(prefix_kernel, heads=heads, hd=hd, c=c, scaling=scaling),
        out_shape=(jax.ShapeDtypeStruct((devices, 2, rows, hd), BF16), stat, stat),
        in_specs=[smem] + [vmem] * 6,
        out_specs=(vmem, vmem, vmem),
        scratch_shapes=[
            pltpu.VMEM((heads * n, hd), BF16),
            pltpu.VMEM((heads * n, hd), BF16),
            pltpu.VMEM((prefix, n), F32),
            pltpu.VMEM((prefix, n), F32),
            pltpu.VMEM((prefix, heads * n), BF16),
            pltpu.VMEM((prefix, heads * n), BF16),
        ],
        compiler_params=pltpu.CompilerParams(vmem_limit_bytes=24 * MIB),
        cost_estimate=pl.CostEstimate(
            flops=8 * heads * n * prefix * hd, bytes_accessed=3 << 20, transcendentals=heads * n * prefix
        ),
        name="prefix_grads",
    )(lengths, q, g, kv, m_own, l_own, d_own)

    parts = lax.all_to_all(grads, ("rollout", "head"), 0, 0, tiled=True)

    dq, own = pl.pallas_call(
        functools.partial(rest_kernel, heads=heads, hd=hd, c=c, scaling=scaling),
        out_shape=(
            jax.ShapeDtypeStruct((n, heads * hd), BF16),
            jax.ShapeDtypeStruct((2, n, hd), BF16),
        ),
        in_specs=[smem] + [vmem] * 7,
        out_specs=(vmem, vmem),
        scratch_shapes=[
            pltpu.VMEM((heads * n, hd), BF16),
            pltpu.VMEM((heads * n, hd), BF16),
            pltpu.VMEM((hd, prefix + n), BF16),
            pltpu.VMEM((n, heads * n), BF16),
            pltpu.VMEM((prefix + n, n), BF16),
        ],
        compiler_params=pltpu.CompilerParams(vmem_limit_bytes=24 * MIB),
        cost_estimate=pl.CostEstimate(
            flops=8 * heads * n * (prefix + n) * hd,
            bytes_accessed=4 << 20,
            transcendentals=heads * n * (prefix + n),
        ),
        name="query_and_own_grads",
    )(lengths, q, g, kv, k_own, v_own, shift, row_dot)

    grad_prefix = pl.pallas_call(
        sum_kernel,
        out_shape=jax.ShapeDtypeStruct((2, rows, head_devices * hd), BF16),
        in_specs=[vmem],
        out_specs=vmem,
        compiler_params=pltpu.CompilerParams(vmem_limit_bytes=4 * MIB),
        name="sum_rollouts",
    )(parts.reshape(rollouts, head_devices, 2, rows, hd))

    return (
        dq.reshape(1, n, 1, heads * hd),
        own.reshape(2, 1, n, 1, hd),
        grad_prefix,
    )


def solution(mesh):
    placed = (
        P(("prompt", "rollout"), None, "head", None),
        P(("prompt", "rollout"), None, "head", None),
        P(("prompt", "rollout"), None, "head", None),
        P(("prompt", "rollout"), None, "head", None),
        P(None, ("prompt", "rollout", "head"), None),
        P(("prompt", "rollout")),
    )
    return jax.shard_map(
        per_device,
        mesh=mesh,
        in_specs=placed,
        out_specs=(
            P(("prompt", "rollout"), None, "head", None),
            P(None, ("prompt", "rollout"), None, "head", None),
            P(None, ("prompt", "rollout", "head"), None),
        ),
        check_vma=False,
    )
```

```python
import functools
import math

import jax
import jax.numpy as jnp
from jax import lax
from jax.experimental import pallas as pl
from jax.experimental.pallas import tpu as pltpu
from jax.sharding import PartitionSpec as P

F32 = jnp.float32
BF16 = jnp.bfloat16
NEG = -1e30
LOG2E = math.log2(math.e)
MIB = 1024 * 1024


def dot_last(a, b):
    return lax.dot_general(a, b, (((1,), (1,)), ((), ())), preferred_element_type=F32)


def dot_plain(a, b):
    return lax.dot_general(a, b, (((1,), (0,)), ((), ())), preferred_element_type=F32)


def fold(x, op):
    parts = [x[i : i + 8] for i in range(0, x.shape[0], 8)]
    while len(parts) > 1:
        parts = [
            op(parts[i], parts[i + 1]) if i + 1 < len(parts) else parts[i]
            for i in range(0, len(parts), 2)
        ]
    return parts[0]


def causal(rows_of_keys, first_key, columns, first_column):
    key = lax.broadcasted_iota(jnp.int32, (rows_of_keys, columns), 0) + first_key
    row = lax.broadcasted_iota(jnp.int32, (rows_of_keys, columns), 1) + first_column
    return key <= row


def own_stats_kernel(
    len_ref, q_ref, g_ref, k_ref, v_ref, m_ref, l_ref, d_ref, qs_ref, gs_ref, *, heads, hd, c
):
    n = q_ref.shape[0]
    half = n // 2
    live = lax.broadcasted_iota(jnp.int32, (n, hd), 0) < len_ref[...]
    for h in range(heads):
        q = q_ref[:, h * hd : (h + 1) * hd]
        g = g_ref[:, h * hd : (h + 1) * hd]
        g = jnp.where(live, g, jnp.zeros_like(g))
        qs_ref[h * n : (h + 1) * n] = q
        gs_ref[h * n : (h + 1) * n] = g
        for b in range(2):
            cols = slice(b * half, (b + 1) * half)
            keys = (b + 1) * half
            s = dot_last(k_ref[0:keys], q[cols]) * c
            s = jnp.where(causal(keys, 0, half, b * half), s, NEG)
            m = jnp.max(fold(s, jnp.maximum), axis=0, keepdims=True)
            p = jnp.exp2(s - m)
            dp = dot_last(v_ref[0:keys], g[cols])
            m_ref[h : h + 1, cols] = m
            l_ref[h : h + 1, cols] = jnp.sum(fold(p, jnp.add), axis=0, keepdims=True)
            d_ref[h : h + 1, cols] = jnp.sum(fold(p * dp, jnp.add), axis=0, keepdims=True)


def prefix_kernel(
    qs_ref, gs_ref, kv_ref, m_ref, l_ref, d_ref,
    send_ref, shift_ref, dot_ref,
    p_ref, dp_ref, w_ref, ds_ref,
    *, heads, hd, c, scaling
):
    n = qs_ref.shape[0] // heads
    devices, _, rows, _ = kv_ref.shape
    prefix = devices * rows
    step, width = 128, 256
    per = step // rows
    chunks = prefix // step

    def block(index, which):
        return kv_ref[index * per : (index + 1) * per, which].reshape(step, hd)

    def spread(x):
        return jnp.broadcast_to(x[None], (step // 8, 8, width)).reshape(step, width)

    kept = []
    for t in range(heads * n // width):
        h = t * width // n
        at = slice(t * width, (t + 1) * width)
        cols = slice(t * width - h * n, (t + 1) * width - h * n)
        q = qs_ref[at]
        g = gs_ref[at]
        m_own = m_ref[h : h + 1, cols]
        m8 = jnp.broadcast_to(m_own, (8, width))
        l8 = jnp.zeros((8, width), F32)
        d8 = jnp.zeros((8, width), F32)
        tops = []
        for i in range(chunks):
            part = slice(i * step, (i + 1) * step)
            s = dot_last(block(i, 0), q) * c
            top = jnp.maximum(m8, fold(s, jnp.maximum))
            p = jnp.exp2(s - spread(top))
            dp = dot_last(block(i, 1), g)
            again = jnp.exp2(m8 - top)
            l8 = l8 * again + fold(p, jnp.add)
            d8 = d8 * again + fold(p * dp, jnp.add)
            m8 = top
            tops.append(top)
            p_ref[part, at] = p
            dp_ref[part, at] = dp
        m = jnp.max(m8, axis=0, keepdims=True)
        again = jnp.exp2(m8 - m)
        again_own = jnp.exp2(m_own - m)
        l = l_ref[h : h + 1, cols] * again_own + jnp.sum(l8 * again, axis=0, keepdims=True)
        d = d_ref[h : h + 1, cols] * again_own + jnp.sum(d8 * again, axis=0, keepdims=True)
        d = d / l
        shift = m + jnp.log2(l)
        shift_ref[h : h + 1, cols] = shift
        dot_ref[h : h + 1, cols] = d
        kept.append((d, [jnp.exp2(top - shift) for top in tops]))
    for t, (d, factors) in enumerate(kept):
        at = slice(t * width, (t + 1) * width)
        for i in range(chunks):
            part = slice(i * step, (i + 1) * step)
            w = p_ref[part, at] * spread(factors[i])
            w_ref[part, at] = w.astype(BF16)
            ds_ref[part, at] = (w * (dp_ref[part, at] - d)).astype(BF16)
    grad_k = dot_plain(ds_ref[...], qs_ref[...]) * scaling
    grad_v = dot_plain(w_ref[...], gs_ref[...])
    send_ref[:, 0] = grad_k.astype(BF16).reshape(devices, rows, hd)
    send_ref[:, 1] = grad_v.astype(BF16).reshape(devices, rows, hd)


def rest_kernel(
    qs_ref, gs_ref, kv_ref, k_ref, v_ref, shift_ref, dot_ref,
    dq_ref, own_ref,
    kt_ref, w_ref, ds_ref,
    *, heads, hd, c, scaling
):
    n = qs_ref.shape[0] // heads
    devices, _, rows, _ = kv_ref.shape
    prefix = devices * rows
    step = 256
    per = step // rows
    half = n // 2
    chunks = prefix // step
    for i in range(chunks):
        k = kv_ref[i * per : (i + 1) * per, 0].reshape(step, hd)
        kt_ref[:, i * step : (i + 1) * step] = k.T
    kt_ref[:, prefix:] = k_ref[...].T
    for h in range(heads):
        shift = shift_ref[h : h + 1]
        d = dot_ref[h : h + 1]
        q = qs_ref[h * n : (h + 1) * n]
        g = gs_ref[h * n : (h + 1) * n]
        for i in range(chunks):
            k = kv_ref[i * per : (i + 1) * per, 0].reshape(step, hd)
            v = kv_ref[i * per : (i + 1) * per, 1].reshape(step, hd)
            w = jnp.exp2(dot_last(k, q) * c - shift)
            ds_ref[i * step : (i + 1) * step] = (w * (dot_last(v, g) - d)).astype(BF16)
        for b in range(2):
            cols = slice(b * half, (b + 1) * half)
            keys = (b + 1) * half
            s = dot_last(k_ref[0:keys], q[cols]) * c
            s = jnp.where(causal(keys, 0, half, b * half), s, NEG)
            w = jnp.exp2(s - shift[:, cols])
            ds = (w * (dot_last(v_ref[0:keys], g[cols]) - d[:, cols])).astype(BF16)
            at = slice(h * n + b * half, h * n + (b + 1) * half)
            w_ref[0:keys, at] = w.astype(BF16)
            ds_ref[prefix : prefix + keys, cols] = ds
            if keys < n:
                empty = jnp.zeros((n - keys, half), BF16)
                w_ref[keys:, at] = empty
                ds_ref[prefix + keys :, cols] = empty
        dqt = dot_plain(kt_ref[...], ds_ref[...]) * scaling
        dq_ref[:, h * hd : (h + 1) * hd] = dqt.T.astype(BF16)
        own = dot_plain(ds_ref[prefix:], q)
        total = own if h == 0 else total + own
    own_ref[0] = (total * scaling).astype(BF16)
    own_ref[1] = dot_plain(w_ref[...], gs_ref[...]).astype(BF16)


def sum_kernel(x_ref, out_ref):
    groups, heads, _, rows, hd = x_ref.shape
    for h in range(heads):
        total = x_ref[0, h].astype(F32)
        for r in range(1, groups):
            total = total + x_ref[r, h].astype(F32)
        out_ref[:, :, h * hd : (h + 1) * hd] = total.astype(BF16)


def per_device(queries, own_keys, own_values, grad_out, prefix_kv, lengths):
    hd = own_keys.shape[3]
    n = queries.shape[1]
    heads = queries.shape[3] // hd
    rollouts = lax.axis_size("rollout")
    head_devices = lax.axis_size("head")
    devices = rollouts * head_devices
    rows = prefix_kv.shape[1]
    prefix = devices * rows
    scaling = 1.0 / math.sqrt(hd)
    c = scaling * LOG2E
    q = queries.reshape(n, heads * hd)
    g = grad_out.reshape(n, heads * hd)
    k_own = own_keys.reshape(n, hd)
    v_own = own_values.reshape(n, hd)

    vmem = pl.BlockSpec(memory_space=pltpu.VMEM)
    stat = jax.ShapeDtypeStruct((heads, n), F32)

    outgoing = jnp.broadcast_to(prefix_kv[None], (rollouts,) + prefix_kv.shape)
    outgoing = outgoing.reshape(rollouts, 2, rows, head_devices, hd).transpose(0, 3, 1, 2, 4)
    outgoing = outgoing.reshape(devices, 2, rows, hd)
    kv = lax.all_to_all(outgoing, ("rollout", "head"), 0, 0, tiled=True)

    stacked = jax.ShapeDtypeStruct((heads * n, hd), BF16)
    m_own, l_own, d_own, q_rows, g_rows = pl.pallas_call(
        functools.partial(own_stats_kernel, heads=heads, hd=hd, c=c),
        out_shape=(stat, stat, stat, stacked, stacked),
        in_specs=[vmem] * 5,
        out_specs=(vmem,) * 5,
        compiler_params=pltpu.CompilerParams(vmem_limit_bytes=12 * MIB),
        cost_estimate=pl.CostEstimate(
            flops=4 * heads * n * n * hd, bytes_accessed=3 << 20, transcendentals=heads * n * n
        ),
        name="own_stats",
    )(lengths.reshape(1, 1), q, g, k_own, v_own)

    grads, shift, row_dot = pl.pallas_call(
        functools.partial(prefix_kernel, heads=heads, hd=hd, c=c, scaling=scaling),
        out_shape=(jax.ShapeDtypeStruct((devices, 2, rows, hd), BF16), stat, stat),
        in_specs=[vmem] * 6,
        out_specs=(vmem, vmem, vmem),
        scratch_shapes=[
            pltpu.VMEM((prefix, heads * n), F32),
            pltpu.VMEM((prefix, heads * n), F32),
            pltpu.VMEM((prefix, heads * n), BF16),
            pltpu.VMEM((prefix, heads * n), BF16),
        ],
        compiler_params=pltpu.CompilerParams(vmem_limit_bytes=28 * MIB),
        cost_estimate=pl.CostEstimate(
            flops=8 * heads * n * prefix * hd, bytes_accessed=3 << 20, transcendentals=heads * n * prefix
        ),
        name="prefix_grads",
    )(q_rows, g_rows, kv, m_own, l_own, d_own)

    parts = lax.all_to_all(grads, ("rollout", "head"), 0, 0, tiled=True)

    dq, own = pl.pallas_call(
        functools.partial(rest_kernel, heads=heads, hd=hd, c=c, scaling=scaling),
        out_shape=(
            jax.ShapeDtypeStruct((n, heads * hd), BF16),
            jax.ShapeDtypeStruct((2, n, hd), BF16),
        ),
        in_specs=[vmem] * 7,
        out_specs=(vmem, vmem),
        scratch_shapes=[
            pltpu.VMEM((hd, prefix + n), BF16),
            pltpu.VMEM((n, heads * n), BF16),
            pltpu.VMEM((prefix + n, n), BF16),
        ],
        compiler_params=pltpu.CompilerParams(vmem_limit_bytes=24 * MIB),
        cost_estimate=pl.CostEstimate(
            flops=8 * heads * n * (prefix + n) * hd,
            bytes_accessed=4 << 20,
            transcendentals=heads * n * (prefix + n),
        ),
        name="query_and_own_grads",
    )(q_rows, g_rows, kv, k_own, v_own, shift, row_dot)

    grad_prefix = pl.pallas_call(
        sum_kernel,
        out_shape=jax.ShapeDtypeStruct((2, rows, head_devices * hd), BF16),
        in_specs=[vmem],
        out_specs=vmem,
        compiler_params=pltpu.CompilerParams(vmem_limit_bytes=4 * MIB),
        name="sum_rollouts",
    )(parts.reshape(rollouts, head_devices, 2, rows, hd))

    return (
        dq.reshape(1, n, 1, heads * hd),
        own.reshape(2, 1, n, 1, hd),
        grad_prefix,
    )


def solution(mesh):
    placed = (
        P(("prompt", "rollout"), None, "head", None),
        P(("prompt", "rollout"), None, "head", None),
        P(("prompt", "rollout"), None, "head", None),
        P(("prompt", "rollout"), None, "head", None),
        P(None, ("prompt", "rollout", "head"), None),
        P(("prompt", "rollout")),
    )
    return jax.shard_map(
        per_device,
        mesh=mesh,
        in_specs=placed,
        out_specs=(
            P(("prompt", "rollout"), None, "head", None),
            P(None, ("prompt", "rollout"), None, "head", None),
            P(None, ("prompt", "rollout", "head"), None),
        ),
        check_vma=False,
    )
```

```python
import functools
import math

import jax
import jax.numpy as jnp
from jax import lax
from jax.experimental import pallas as pl
from jax.experimental.pallas import tpu as pltpu
from jax.sharding import PartitionSpec as P

F32 = jnp.float32
BF16 = jnp.bfloat16
NEG = -1e30
LOG2E = math.log2(math.e)
MIB = 1024 * 1024


def dot_last(a, b):
    return lax.dot_general(a, b, (((1,), (1,)), ((), ())), preferred_element_type=F32)


def dot_plain(a, b):
    return lax.dot_general(a, b, (((1,), (0,)), ((), ())), preferred_element_type=F32)


def fold(x, op):
    parts = [x[i : i + 8] for i in range(0, x.shape[0], 8)]
    while len(parts) > 1:
        parts = [
            op(parts[i], parts[i + 1]) if i + 1 < len(parts) else parts[i]
            for i in range(0, len(parts), 2)
        ]
    return parts[0]


def causal(rows_of_keys, first_key, columns, first_column):
    key = lax.broadcasted_iota(jnp.int32, (rows_of_keys, columns), 0) + first_key
    row = lax.broadcasted_iota(jnp.int32, (rows_of_keys, columns), 1) + first_column
    return key <= row


def own_stats_kernel(
    len_ref, q_ref, g_ref, k_ref, v_ref, m_ref, l_ref, d_ref, qs_ref, gs_ref, *, heads, hd, c
):
    n = q_ref.shape[0]
    half = n // 2
    live = lax.broadcasted_iota(jnp.int32, (n, hd), 0) < len_ref[...]
    for h in range(heads):
        q = q_ref[:, h * hd : (h + 1) * hd]
        g = g_ref[:, h * hd : (h + 1) * hd]
        g = jnp.where(live, g, jnp.zeros_like(g))
        qs_ref[h * n : (h + 1) * n] = q
        gs_ref[h * n : (h + 1) * n] = g
        for b in range(2):
            cols = slice(b * half, (b + 1) * half)
            keys = (b + 1) * half
            s = dot_last(k_ref[0:keys], q[cols]) * c
            s = jnp.where(causal(keys, 0, half, b * half), s, NEG)
            m = jnp.max(fold(s, jnp.maximum), axis=0, keepdims=True)
            p = jnp.exp2(s - m)
            dp = dot_last(v_ref[0:keys], g[cols])
            m_ref[h : h + 1, cols] = m
            l_ref[h : h + 1, cols] = jnp.sum(fold(p, jnp.add), axis=0, keepdims=True)
            d_ref[h : h + 1, cols] = jnp.sum(fold(p * dp, jnp.add), axis=0, keepdims=True)


def prefix_kernel(
    qs_ref, gs_ref, kv_ref, m_ref, l_ref, d_ref,
    send_ref, shift_ref, dot_ref,
    p_ref, dp_ref, w_ref, ds_ref, inv_ref, total_ref,
    *, heads, hd, c, scaling
):
    n = qs_ref.shape[0] // heads
    devices, _, rows, _ = kv_ref.shape
    prefix = devices * rows
    step, width, last = 256, 256, 512
    chunks = prefix // step
    tiles = []
    for t in range(heads * n // width):
        h = t * width // n
        first = t * width - h * n
        tiles.append((slice(h, h + 1), slice(first, first + width), slice(t * width, (t + 1) * width)))

    def block(index, which):
        per = step // rows
        return kv_ref[index * per : (index + 1) * per, which].reshape(step, hd)

    def weigh(exact):
        for head, cols, at in tiles:
            q = qs_ref[at]
            g = gs_ref[at]
            m = m_ref[head, cols]
            l = l_ref[head, cols]
            d = d_ref[head, cols]
            if exact:
                own = m
                for i in range(chunks):
                    top = fold(dot_last(block(i, 0), q) * c, jnp.maximum)
                    m = jnp.maximum(m, jnp.max(top, axis=0, keepdims=True))
                again = jnp.exp2(own - m)
                l = l * again
                d = d * again
            l8 = jnp.zeros((8, width), F32)
            d8 = jnp.zeros((8, width), F32)
            for i in range(chunks):
                part = slice(i * step, (i + 1) * step)
                p = jnp.exp2(dot_last(block(i, 0), q) * c - m)
                dp = dot_last(block(i, 1), g)
                l8 = l8 + fold(p, jnp.add)
                d8 = d8 + fold(p * dp, jnp.add)
                p_ref[part, at] = p
                dp_ref[part, at] = dp
            l = l + jnp.sum(l8, axis=0, keepdims=True)
            d = d + jnp.sum(d8, axis=0, keepdims=True)
            inv = 1.0 / l
            total_ref[head, cols] = l
            inv_ref[head, cols] = inv
            shift_ref[head, cols] = m + jnp.log2(l)
            dot_ref[head, cols] = d * inv

    weigh(False)
    fits = jnp.max(total_ref[...]) < 2.0**60

    @pl.when(jnp.logical_not(fits))
    def _():
        weigh(True)

    for e in range(prefix // last):
        for head, cols, at in tiles:
            inv = inv_ref[head, cols]
            d = dot_ref[head, cols]
            for i in range(last // step):
                part = slice(e * last + i * step, e * last + (i + 1) * step)
                w = p_ref[part, at] * inv
                w_ref[part, at] = w.astype(BF16)
                ds_ref[part, at] = (w * (dp_ref[part, at] - d)).astype(BF16)
        part = slice(e * last, (e + 1) * last)
        owners = slice(e * last // rows, (e + 1) * last // rows)
        shape = (last // rows, rows, hd)
        grad_v = dot_plain(w_ref[part], gs_ref[...])
        send_ref[owners, 1] = grad_v.astype(BF16).reshape(shape)
        grad_k = dot_plain(ds_ref[part], qs_ref[...]) * scaling
        send_ref[owners, 0] = grad_k.astype(BF16).reshape(shape)


def rest_kernel(
    qs_ref, gs_ref, kv_ref, k_ref, v_ref, shift_ref, dot_ref,
    dq_ref, own_ref,
    kt_ref, w_ref, ds_ref,
    *, heads, hd, c, scaling
):
    n = qs_ref.shape[0] // heads
    devices, _, rows, _ = kv_ref.shape
    prefix = devices * rows
    step = 256
    per = step // rows
    half = n // 2
    chunks = prefix // step
    for i in range(chunks):
        k = kv_ref[i * per : (i + 1) * per, 0].reshape(step, hd)
        kt_ref[:, i * step : (i + 1) * step] = k.T
    kt_ref[:, prefix:] = k_ref[...].T
    for h in range(heads):
        shift = shift_ref[h : h + 1]
        d = dot_ref[h : h + 1]
        q = qs_ref[h * n : (h + 1) * n]
        g = gs_ref[h * n : (h + 1) * n]
        for i in range(chunks):
            k = kv_ref[i * per : (i + 1) * per, 0].reshape(step, hd)
            v = kv_ref[i * per : (i + 1) * per, 1].reshape(step, hd)
            w = jnp.exp2(dot_last(k, q) * c - shift)
            ds_ref[i * step : (i + 1) * step] = (w * (dot_last(v, g) - d)).astype(BF16)
        for b in range(2):
            cols = slice(b * half, (b + 1) * half)
            keys = (b + 1) * half
            s = dot_last(k_ref[0:keys], q[cols]) * c
            s = jnp.where(causal(keys, 0, half, b * half), s, NEG)
            w = jnp.exp2(s - shift[:, cols])
            ds = (w * (dot_last(v_ref[0:keys], g[cols]) - d[:, cols])).astype(BF16)
            at = slice(h * n + b * half, h * n + (b + 1) * half)
            w_ref[0:keys, at] = w.astype(BF16)
            ds_ref[prefix : prefix + keys, cols] = ds
            if keys < n:
                empty = jnp.zeros((n - keys, half), BF16)
                w_ref[keys:, at] = empty
                ds_ref[prefix + keys :, cols] = empty
        dqt = dot_plain(kt_ref[...], ds_ref[...]) * scaling
        dq_ref[:, h * hd : (h + 1) * hd] = dqt.T.astype(BF16)
        own = dot_plain(ds_ref[prefix:], q)
        total = own if h == 0 else total + own
    own_ref[0] = (total * scaling).astype(BF16)
    own_ref[1] = dot_plain(w_ref[...], gs_ref[...]).astype(BF16)


def sum_kernel(x_ref, out_ref):
    groups, heads, _, rows, hd = x_ref.shape
    for h in range(heads):
        total = x_ref[0, h].astype(F32)
        for r in range(1, groups):
            total = total + x_ref[r, h].astype(F32)
        out_ref[:, :, h * hd : (h + 1) * hd] = total.astype(BF16)


def per_device(queries, own_keys, own_values, grad_out, prefix_kv, lengths):
    hd = own_keys.shape[3]
    n = queries.shape[1]
    heads = queries.shape[3] // hd
    rollouts = lax.axis_size("rollout")
    head_devices = lax.axis_size("head")
    devices = rollouts * head_devices
    rows = prefix_kv.shape[1]
    prefix = devices * rows
    scaling = 1.0 / math.sqrt(hd)
    c = scaling * LOG2E
    q = queries.reshape(n, heads * hd)
    g = grad_out.reshape(n, heads * hd)
    k_own = own_keys.reshape(n, hd)
    v_own = own_values.reshape(n, hd)

    vmem = pl.BlockSpec(memory_space=pltpu.VMEM)
    stat = jax.ShapeDtypeStruct((heads, n), F32)

    outgoing = jnp.broadcast_to(prefix_kv[None], (rollouts,) + prefix_kv.shape)
    outgoing = outgoing.reshape(rollouts, 2, rows, head_devices, hd).transpose(0, 3, 1, 2, 4)
    outgoing = outgoing.reshape(devices, 2, rows, hd)
    kv = lax.all_to_all(outgoing, ("rollout", "head"), 0, 0, tiled=True)

    stacked = jax.ShapeDtypeStruct((heads * n, hd), BF16)
    m_own, l_own, d_own, q_rows, g_rows = pl.pallas_call(
        functools.partial(own_stats_kernel, heads=heads, hd=hd, c=c),
        out_shape=(stat, stat, stat, stacked, stacked),
        in_specs=[vmem] * 5,
        out_specs=(vmem,) * 5,
        compiler_params=pltpu.CompilerParams(vmem_limit_bytes=12 * MIB),
        cost_estimate=pl.CostEstimate(
            flops=4 * heads * n * n * hd, bytes_accessed=3 << 20, transcendentals=heads * n * n
        ),
        name="own_stats",
    )(lengths.reshape(1, 1), q, g, k_own, v_own)

    grads, shift, row_dot = pl.pallas_call(
        functools.partial(prefix_kernel, heads=heads, hd=hd, c=c, scaling=scaling),
        out_shape=(jax.ShapeDtypeStruct((devices, 2, rows, hd), BF16), stat, stat),
        in_specs=[vmem] * 6,
        out_specs=(vmem, vmem, vmem),
        scratch_shapes=[
            pltpu.VMEM((prefix, heads * n), F32),
            pltpu.VMEM((prefix, heads * n), F32),
            pltpu.VMEM((prefix, heads * n), BF16),
            pltpu.VMEM((prefix, heads * n), BF16),
            pltpu.VMEM((heads, n), F32),
            pltpu.VMEM((heads, n), F32),
        ],
        compiler_params=pltpu.CompilerParams(vmem_limit_bytes=28 * MIB),
        cost_estimate=pl.CostEstimate(
            flops=8 * heads * n * prefix * hd, bytes_accessed=3 << 20, transcendentals=heads * n * prefix
        ),
        name="prefix_grads",
    )(q_rows, g_rows, kv, m_own, l_own, d_own)

    parts = lax.all_to_all(grads, ("rollout", "head"), 0, 0, tiled=True)

    dq, own = pl.pallas_call(
        functools.partial(rest_kernel, heads=heads, hd=hd, c=c, scaling=scaling),
        out_shape=(
            jax.ShapeDtypeStruct((n, heads * hd), BF16),
            jax.ShapeDtypeStruct((2, n, hd), BF16),
        ),
        in_specs=[vmem] * 7,
        out_specs=(vmem, vmem),
        scratch_shapes=[
            pltpu.VMEM((hd, prefix + n), BF16),
            pltpu.VMEM((n, heads * n), BF16),
            pltpu.VMEM((prefix + n, n), BF16),
        ],
        compiler_params=pltpu.CompilerParams(vmem_limit_bytes=24 * MIB),
        cost_estimate=pl.CostEstimate(
            flops=8 * heads * n * (prefix + n) * hd,
            bytes_accessed=4 << 20,
            transcendentals=heads * n * (prefix + n),
        ),
        name="query_and_own_grads",
    )(q_rows, g_rows, kv, k_own, v_own, shift, row_dot)

    grad_prefix = pl.pallas_call(
        sum_kernel,
        out_shape=jax.ShapeDtypeStruct((2, rows, head_devices * hd), BF16),
        in_specs=[vmem],
        out_specs=vmem,
        compiler_params=pltpu.CompilerParams(vmem_limit_bytes=4 * MIB),
        name="sum_rollouts",
    )(parts.reshape(rollouts, head_devices, 2, rows, hd))

    return (
        dq.reshape(1, n, 1, heads * hd),
        own.reshape(2, 1, n, 1, hd),
        grad_prefix,
    )


def solution(mesh):
    placed = (
        P(("prompt", "rollout"), None, "head", None),
        P(("prompt", "rollout"), None, "head", None),
        P(("prompt", "rollout"), None, "head", None),
        P(("prompt", "rollout"), None, "head", None),
        P(None, ("prompt", "rollout", "head"), None),
        P(("prompt", "rollout")),
    )
    return jax.shard_map(
        per_device,
        mesh=mesh,
        in_specs=placed,
        out_specs=(
            P(("prompt", "rollout"), None, "head", None),
            P(None, ("prompt", "rollout"), None, "head", None),
            P(None, ("prompt", "rollout", "head"), None),
        ),
        check_vma=False,
    )
```

```python
import functools
import math

import jax
import jax.numpy as jnp
from jax import lax
from jax.experimental import pallas as pl
from jax.experimental.pallas import tpu as pltpu
from jax.sharding import PartitionSpec as P

F32 = jnp.float32
BF16 = jnp.bfloat16
NEG = -1e30
LOG2E = math.log2(math.e)
MIB = 1024 * 1024


def dot_last(a, b):
    return lax.dot_general(a, b, (((1,), (1,)), ((), ())), preferred_element_type=F32)


def dot_plain(a, b):
    return lax.dot_general(a, b, (((1,), (0,)), ((), ())), preferred_element_type=F32)


def fold(x, op):
    parts = [x[i : i + 8] for i in range(0, x.shape[0], 8)]
    while len(parts) > 1:
        parts = [
            op(parts[i], parts[i + 1]) if i + 1 < len(parts) else parts[i]
            for i in range(0, len(parts), 2)
        ]
    return parts[0]


def causal(rows_of_keys, first_key, columns, first_column):
    key = lax.broadcasted_iota(jnp.int32, (rows_of_keys, columns), 0) + first_key
    row = lax.broadcasted_iota(jnp.int32, (rows_of_keys, columns), 1) + first_column
    return key <= row


def own_stats_kernel(
    len_ref, q_ref, g_ref, k_ref, v_ref, m_ref, l_ref, d_ref, qs_ref, gs_ref, *, heads, hd, c
):
    n = q_ref.shape[0]
    half = n // 2
    live = lax.broadcasted_iota(jnp.int32, (n, hd), 0) < len_ref[...]
    for h in range(heads):
        q = q_ref[:, h * hd : (h + 1) * hd]
        g = g_ref[:, h * hd : (h + 1) * hd]
        g = jnp.where(live, g, jnp.zeros_like(g))
        qs_ref[h * n : (h + 1) * n] = q
        gs_ref[h * n : (h + 1) * n] = g
        for b in range(2):
            cols = slice(b * half, (b + 1) * half)
            keys = (b + 1) * half
            s = dot_last(k_ref[0:keys], q[cols]) * c
            s = jnp.where(causal(keys, 0, half, b * half), s, NEG)
            m = jnp.max(fold(s, jnp.maximum), axis=0, keepdims=True)
            p = jnp.exp2(s - m)
            dp = dot_last(v_ref[0:keys], g[cols])
            m_ref[h : h + 1, cols] = m
            l_ref[h : h + 1, cols] = jnp.sum(fold(p, jnp.add), axis=0, keepdims=True)
            d_ref[h : h + 1, cols] = jnp.sum(fold(p * dp, jnp.add), axis=0, keepdims=True)


def prefix_kernel(
    qs_ref, gs_ref, kv_ref, m_ref, l_ref, d_ref,
    send_ref, shift_ref, dot_ref,
    p_ref, dp_ref, w_ref, ds_ref, inv_ref, total_ref,
    *, heads, hd, c, scaling
):
    n = qs_ref.shape[0] // heads
    devices, _, rows, _ = kv_ref.shape
    prefix = devices * rows
    step, width, last = 256, 256, 512
    chunks = prefix // step
    tiles = []
    for t in range(heads * n // width):
        h = t * width // n
        first = t * width - h * n
        tiles.append((slice(h, h + 1), slice(first, first + width), slice(t * width, (t + 1) * width)))

    def block(index, which):
        per = step // rows
        return kv_ref[index * per : (index + 1) * per, which].reshape(step, hd)

    def weigh(exact):
        for head, cols, at in tiles:
            q = qs_ref[at]
            g = gs_ref[at]
            m = m_ref[head, cols]
            l = l_ref[head, cols]
            d = d_ref[head, cols]
            if exact:
                own = m
                for i in range(chunks):
                    top = fold(dot_last(block(i, 0), q) * c, jnp.maximum)
                    m = jnp.maximum(m, jnp.max(top, axis=0, keepdims=True))
                again = jnp.exp2(own - m)
                l = l * again
                d = d * again
            l8 = jnp.zeros((8, width), F32)
            d8 = jnp.zeros((8, width), F32)
            for i in range(chunks):
                part = slice(i * step, (i + 1) * step)
                p = jnp.exp2(dot_last(block(i, 0), q) * c - m)
                l8 = l8 + fold(p, jnp.add)
                p_ref[part, at] = p
            for i in range(chunks):
                part = slice(i * step, (i + 1) * step)
                dp = dot_last(block(i, 1), g)
                d8 = d8 + fold(p_ref[part, at] * dp, jnp.add)
                dp_ref[part, at] = dp
            l = l + jnp.sum(l8, axis=0, keepdims=True)
            d = d + jnp.sum(d8, axis=0, keepdims=True)
            inv = 1.0 / l
            total_ref[head, cols] = l
            inv_ref[head, cols] = inv
            shift_ref[head, cols] = m + jnp.log2(l)
            dot_ref[head, cols] = d * inv

    weigh(False)
    fits = jnp.max(total_ref[...]) < 2.0**60

    @pl.when(jnp.logical_not(fits))
    def _():
        weigh(True)

    for e in range(prefix // last):
        for head, cols, at in tiles:
            inv = inv_ref[head, cols]
            d = dot_ref[head, cols]
            for i in range(last // step):
                part = slice(e * last + i * step, e * last + (i + 1) * step)
                w = p_ref[part, at] * inv
                w_ref[part, at] = w.astype(BF16)
                ds_ref[part, at] = (w * (dp_ref[part, at] - d)).astype(BF16)
        part = slice(e * last, (e + 1) * last)
        owners = slice(e * last // rows, (e + 1) * last // rows)
        shape = (last // rows, rows, hd)
        grad_v = dot_plain(w_ref[part], gs_ref[...])
        send_ref[owners, 1] = grad_v.astype(BF16).reshape(shape)
        grad_k = dot_plain(ds_ref[part], qs_ref[...]) * scaling
        send_ref[owners, 0] = grad_k.astype(BF16).reshape(shape)


def rest_kernel(
    qs_ref, gs_ref, kv_ref, k_ref, v_ref, shift_ref, dot_ref,
    dq_ref, own_ref,
    kt_ref, w_ref, ds_ref,
    *, heads, hd, c, scaling
):
    n = qs_ref.shape[0] // heads
    devices, _, rows, _ = kv_ref.shape
    prefix = devices * rows
    step = 256
    per = step // rows
    half = n // 2
    chunks = prefix // step
    for i in range(chunks):
        k = kv_ref[i * per : (i + 1) * per, 0].reshape(step, hd)
        kt_ref[:, i * step : (i + 1) * step] = k.T
    kt_ref[:, prefix:] = k_ref[...].T
    for h in range(heads):
        shift = shift_ref[h : h + 1]
        d = dot_ref[h : h + 1]
        q = qs_ref[h * n : (h + 1) * n]
        g = gs_ref[h * n : (h + 1) * n]
        for i in range(chunks):
            k = kv_ref[i * per : (i + 1) * per, 0].reshape(step, hd)
            v = kv_ref[i * per : (i + 1) * per, 1].reshape(step, hd)
            w = jnp.exp2(dot_last(k, q) * c - shift)
            ds_ref[i * step : (i + 1) * step] = (w * (dot_last(v, g) - d)).astype(BF16)
        for b in range(2):
            cols = slice(b * half, (b + 1) * half)
            keys = (b + 1) * half
            s = dot_last(k_ref[0:keys], q[cols]) * c
            s = jnp.where(causal(keys, 0, half, b * half), s, NEG)
            w = jnp.exp2(s - shift[:, cols])
            ds = (w * (dot_last(v_ref[0:keys], g[cols]) - d[:, cols])).astype(BF16)
            at = slice(h * n + b * half, h * n + (b + 1) * half)
            w_ref[0:keys, at] = w.astype(BF16)
            ds_ref[prefix : prefix + keys, cols] = ds
            if keys < n:
                empty = jnp.zeros((n - keys, half), BF16)
                w_ref[keys:, at] = empty
                ds_ref[prefix + keys :, cols] = empty
        dqt = dot_plain(kt_ref[...], ds_ref[...]) * scaling
        dq_ref[:, h * hd : (h + 1) * hd] = dqt.T.astype(BF16)
        own = dot_plain(ds_ref[prefix:], q)
        total = own if h == 0 else total + own
    own_ref[0] = (total * scaling).astype(BF16)
    own_ref[1] = dot_plain(w_ref[...], gs_ref[...]).astype(BF16)


def sum_kernel(x_ref, out_ref):
    groups, heads, _, rows, hd = x_ref.shape
    for h in range(heads):
        total = x_ref[0, h].astype(F32)
        for r in range(1, groups):
            total = total + x_ref[r, h].astype(F32)
        out_ref[:, :, h * hd : (h + 1) * hd] = total.astype(BF16)


def per_device(queries, own_keys, own_values, grad_out, prefix_kv, lengths):
    hd = own_keys.shape[3]
    n = queries.shape[1]
    heads = queries.shape[3] // hd
    rollouts = lax.axis_size("rollout")
    head_devices = lax.axis_size("head")
    devices = rollouts * head_devices
    rows = prefix_kv.shape[1]
    prefix = devices * rows
    scaling = 1.0 / math.sqrt(hd)
    c = scaling * LOG2E
    q = queries.reshape(n, heads * hd)
    g = grad_out.reshape(n, heads * hd)
    k_own = own_keys.reshape(n, hd)
    v_own = own_values.reshape(n, hd)

    vmem = pl.BlockSpec(memory_space=pltpu.VMEM)
    stat = jax.ShapeDtypeStruct((heads, n), F32)

    outgoing = jnp.broadcast_to(prefix_kv[None], (rollouts,) + prefix_kv.shape)
    outgoing = outgoing.reshape(rollouts, 2, rows, head_devices, hd).transpose(0, 3, 1, 2, 4)
    outgoing = outgoing.reshape(devices, 2, rows, hd)
    kv = lax.all_to_all(outgoing, ("rollout", "head"), 0, 0, tiled=True)

    stacked = jax.ShapeDtypeStruct((heads * n, hd), BF16)
    m_own, l_own, d_own, q_rows, g_rows = pl.pallas_call(
        functools.partial(own_stats_kernel, heads=heads, hd=hd, c=c),
        out_shape=(stat, stat, stat, stacked, stacked),
        in_specs=[vmem] * 5,
        out_specs=(vmem,) * 5,
        compiler_params=pltpu.CompilerParams(vmem_limit_bytes=12 * MIB),
        cost_estimate=pl.CostEstimate(
            flops=4 * heads * n * n * hd, bytes_accessed=3 << 20, transcendentals=heads * n * n
        ),
        name="own_stats",
    )(lengths.reshape(1, 1), q, g, k_own, v_own)

    grads, shift, row_dot = pl.pallas_call(
        functools.partial(prefix_kernel, heads=heads, hd=hd, c=c, scaling=scaling),
        out_shape=(jax.ShapeDtypeStruct((devices, 2, rows, hd), BF16), stat, stat),
        in_specs=[vmem] * 6,
        out_specs=(vmem, vmem, vmem),
        scratch_shapes=[
            pltpu.VMEM((prefix, heads * n), F32),
            pltpu.VMEM((prefix, heads * n), F32),
            pltpu.VMEM((prefix, heads * n), BF16),
            pltpu.VMEM((prefix, heads * n), BF16),
            pltpu.VMEM((heads, n), F32),
            pltpu.VMEM((heads, n), F32),
        ],
        compiler_params=pltpu.CompilerParams(vmem_limit_bytes=28 * MIB),
        cost_estimate=pl.CostEstimate(
            flops=8 * heads * n * prefix * hd, bytes_accessed=3 << 20, transcendentals=heads * n * prefix
        ),
        name="prefix_grads",
    )(q_rows, g_rows, kv, m_own, l_own, d_own)

    parts = lax.all_to_all(grads, ("rollout", "head"), 0, 0, tiled=True)

    dq, own = pl.pallas_call(
        functools.partial(rest_kernel, heads=heads, hd=hd, c=c, scaling=scaling),
        out_shape=(
            jax.ShapeDtypeStruct((n, heads * hd), BF16),
            jax.ShapeDtypeStruct((2, n, hd), BF16),
        ),
        in_specs=[vmem] * 7,
        out_specs=(vmem, vmem),
        scratch_shapes=[
            pltpu.VMEM((hd, prefix + n), BF16),
            pltpu.VMEM((n, heads * n), BF16),
            pltpu.VMEM((prefix + n, n), BF16),
        ],
        compiler_params=pltpu.CompilerParams(vmem_limit_bytes=24 * MIB),
        cost_estimate=pl.CostEstimate(
            flops=8 * heads * n * (prefix + n) * hd,
            bytes_accessed=4 << 20,
            transcendentals=heads * n * (prefix + n),
        ),
        name="query_and_own_grads",
    )(q_rows, g_rows, kv, k_own, v_own, shift, row_dot)

    grad_prefix = pl.pallas_call(
        sum_kernel,
        out_shape=jax.ShapeDtypeStruct((2, rows, head_devices * hd), BF16),
        in_specs=[vmem],
        out_specs=vmem,
        compiler_params=pltpu.CompilerParams(vmem_limit_bytes=4 * MIB),
        name="sum_rollouts",
    )(parts.reshape(rollouts, head_devices, 2, rows, hd))

    return (
        dq.reshape(1, n, 1, heads * hd),
        own.reshape(2, 1, n, 1, hd),
        grad_prefix,
    )


def solution(mesh):
    placed = (
        P(("prompt", "rollout"), None, "head", None),
        P(("prompt", "rollout"), None, "head", None),
        P(("prompt", "rollout"), None, "head", None),
        P(("prompt", "rollout"), None, "head", None),
        P(None, ("prompt", "rollout", "head"), None),
        P(("prompt", "rollout")),
    )
    return jax.shard_map(
        per_device,
        mesh=mesh,
        in_specs=placed,
        out_specs=(
            P(("prompt", "rollout"), None, "head", None),
            P(None, ("prompt", "rollout"), None, "head", None),
            P(None, ("prompt", "rollout", "head"), None),
        ),
        check_vma=False,
    )
```

```python
import functools
import math

import jax
import jax.numpy as jnp
from jax import lax
from jax.experimental import pallas as pl
from jax.experimental.pallas import tpu as pltpu
from jax.sharding import PartitionSpec as P

F32 = jnp.float32
BF16 = jnp.bfloat16
NEG = -1e30
LOG2E = math.log2(math.e)
MIB = 1024 * 1024


def dot_last(a, b):
    return lax.dot_general(a, b, (((1,), (1,)), ((), ())), preferred_element_type=F32)


def dot_plain(a, b):
    return lax.dot_general(a, b, (((1,), (0,)), ((), ())), preferred_element_type=F32)


def fold(x, op):
    parts = [x[i : i + 8] for i in range(0, x.shape[0], 8)]
    while len(parts) > 1:
        parts = [
            op(parts[i], parts[i + 1]) if i + 1 < len(parts) else parts[i]
            for i in range(0, len(parts), 2)
        ]
    return parts[0]


def causal(rows_of_keys, first_key, columns, first_column):
    key = lax.broadcasted_iota(jnp.int32, (rows_of_keys, columns), 0) + first_key
    row = lax.broadcasted_iota(jnp.int32, (rows_of_keys, columns), 1) + first_column
    return key <= row


def own_stats_kernel(
    len_ref, q_ref, g_ref, k_ref, v_ref, m_ref, l_ref, d_ref, qs_ref, gs_ref, *, heads, hd, c
):
    n = q_ref.shape[0]
    half = n // 2
    live = lax.broadcasted_iota(jnp.int32, (n, hd), 0) < len_ref[...]
    for h in range(heads):
        q = q_ref[:, h * hd : (h + 1) * hd]
        g = g_ref[:, h * hd : (h + 1) * hd]
        g = jnp.where(live, g, jnp.zeros_like(g))
        qs_ref[h * n : (h + 1) * n] = q
        gs_ref[h * n : (h + 1) * n] = g
        for b in range(2):
            cols = slice(b * half, (b + 1) * half)
            keys = (b + 1) * half
            s = dot_last(k_ref[0:keys], q[cols]) * c
            s = jnp.where(causal(keys, 0, half, b * half), s, NEG)
            m = jnp.max(fold(s, jnp.maximum), axis=0, keepdims=True)
            p = jnp.exp2(s - m)
            dp = dot_last(v_ref[0:keys], g[cols])
            m_ref[h : h + 1, cols] = m
            l_ref[h : h + 1, cols] = jnp.sum(fold(p, jnp.add), axis=0, keepdims=True)
            d_ref[h : h + 1, cols] = jnp.sum(fold(p * dp, jnp.add), axis=0, keepdims=True)


def prefix_kernel(
    qs_ref, gs_ref, kv_ref, m_ref, l_ref, d_ref,
    send_ref, shift_ref, dot_ref,
    p_ref, dp_ref, w_ref, ds_ref, inv_ref, total_ref,
    *, heads, hd, c, scaling
):
    n = qs_ref.shape[0] // heads
    devices, _, rows, _ = kv_ref.shape
    prefix = devices * rows
    step, width, last = 256, 256, 512
    chunks = prefix // step
    tiles = []
    for t in range(heads * n // width):
        h = t * width // n
        first = t * width - h * n
        tiles.append((slice(h, h + 1), slice(first, first + width), slice(t * width, (t + 1) * width)))

    def block(index, which):
        per = step // rows
        return kv_ref[index * per : (index + 1) * per, which].reshape(step, hd)

    def weigh(exact):
        for head, cols, at in tiles:
            q = qs_ref[at]
            g = gs_ref[at]
            m = m_ref[head, cols]
            l = l_ref[head, cols]
            d = d_ref[head, cols]
            if exact:
                own = m
                for i in range(chunks):
                    top = fold(dot_last(block(i, 0), q) * c, jnp.maximum)
                    m = jnp.maximum(m, jnp.max(top, axis=0, keepdims=True))
                again = jnp.exp2(own - m)
                l = l * again
                d = d * again
            l8 = jnp.zeros((8, width), F32)
            d8 = jnp.zeros((8, width), F32)
            for i in range(chunks):
                part = slice(i * step, (i + 1) * step)
                p = jnp.exp2(dot_last(block(i, 0), q) * c - m)
                l8 = l8 + fold(p, jnp.add)
                p_ref[part, at] = p
            for i in range(chunks):
                part = slice(i * step, (i + 1) * step)
                dp = dot_last(block(i, 1), g)
                d8 = d8 + fold(p_ref[part, at] * dp, jnp.add)
                dp_ref[part, at] = dp
            l = l + jnp.sum(l8, axis=0, keepdims=True)
            d = d + jnp.sum(d8, axis=0, keepdims=True)
            inv = 1.0 / l
            total_ref[head, cols] = l
            inv_ref[head, cols] = inv
            shift_ref[head, cols] = m + jnp.log2(l)
            dot_ref[head, cols] = d * inv

    weigh(False)
    fits = jnp.max(total_ref[...]) < 2.0**60

    @pl.when(jnp.logical_not(fits))
    def _():
        weigh(True)

    for e in range(prefix // last):
        for head, cols, at in tiles:
            inv = inv_ref[head, cols]
            for i in range(last // step):
                part = slice(e * last + i * step, e * last + (i + 1) * step)
                w_ref[part, at] = (p_ref[part, at] * inv).astype(BF16)
        part = slice(e * last, (e + 1) * last)
        owners = slice(e * last // rows, (e + 1) * last // rows)
        shape = (last // rows, rows, hd)
        grad_v = dot_plain(w_ref[part], gs_ref[...])
        send_ref[owners, 1] = grad_v.astype(BF16).reshape(shape)
    for e in range(prefix // last):
        for head, cols, at in tiles:
            inv = inv_ref[head, cols]
            d = dot_ref[head, cols]
            for i in range(last // step):
                part = slice(e * last + i * step, e * last + (i + 1) * step)
                ds_ref[part, at] = (p_ref[part, at] * inv * (dp_ref[part, at] - d)).astype(BF16)
        part = slice(e * last, (e + 1) * last)
        owners = slice(e * last // rows, (e + 1) * last // rows)
        grad_k = dot_plain(ds_ref[part], qs_ref[...]) * scaling
        send_ref[owners, 0] = grad_k.astype(BF16).reshape(shape)


def rest_kernel(
    qs_ref, gs_ref, kv_ref, k_ref, v_ref, shift_ref, dot_ref,
    dq_ref, own_ref,
    kt_ref, w_ref, ds_ref,
    *, heads, hd, c, scaling
):
    n = qs_ref.shape[0] // heads
    devices, _, rows, _ = kv_ref.shape
    prefix = devices * rows
    step = 256
    per = step // rows
    half = n // 2
    chunks = prefix // step
    for i in range(chunks):
        k = kv_ref[i * per : (i + 1) * per, 0].reshape(step, hd)
        kt_ref[:, i * step : (i + 1) * step] = k.T
    kt_ref[:, prefix:] = k_ref[...].T
    for h in range(heads):
        shift = shift_ref[h : h + 1]
        d = dot_ref[h : h + 1]
        q = qs_ref[h * n : (h + 1) * n]
        g = gs_ref[h * n : (h + 1) * n]
        for i in range(chunks):
            k = kv_ref[i * per : (i + 1) * per, 0].reshape(step, hd)
            v = kv_ref[i * per : (i + 1) * per, 1].reshape(step, hd)
            w = jnp.exp2(dot_last(k, q) * c - shift)
            ds_ref[i * step : (i + 1) * step] = (w * (dot_last(v, g) - d)).astype(BF16)
        for b in range(2):
            cols = slice(b * half, (b + 1) * half)
            keys = (b + 1) * half
            s = dot_last(k_ref[0:keys], q[cols]) * c
            s = jnp.where(causal(keys, 0, half, b * half), s, NEG)
            w = jnp.exp2(s - shift[:, cols])
            ds = (w * (dot_last(v_ref[0:keys], g[cols]) - d[:, cols])).astype(BF16)
            at = slice(h * n + b * half, h * n + (b + 1) * half)
            w_ref[0:keys, at] = w.astype(BF16)
            ds_ref[prefix : prefix + keys, cols] = ds
            if keys < n:
                empty = jnp.zeros((n - keys, half), BF16)
                w_ref[keys:, at] = empty
                ds_ref[prefix + keys :, cols] = empty
        dqt = dot_plain(kt_ref[...], ds_ref[...]) * scaling
        dq_ref[:, h * hd : (h + 1) * hd] = dqt.T.astype(BF16)
        own = dot_plain(ds_ref[prefix:], q)
        total = own if h == 0 else total + own
    own_ref[0] = (total * scaling).astype(BF16)
    own_ref[1] = dot_plain(w_ref[...], gs_ref[...]).astype(BF16)


def sum_kernel(x_ref, out_ref):
    groups, heads, _, rows, hd = x_ref.shape
    for h in range(heads):
        total = x_ref[0, h].astype(F32)
        for r in range(1, groups):
            total = total + x_ref[r, h].astype(F32)
        out_ref[:, :, h * hd : (h + 1) * hd] = total.astype(BF16)


def per_device(queries, own_keys, own_values, grad_out, prefix_kv, lengths):
    hd = own_keys.shape[3]
    n = queries.shape[1]
    heads = queries.shape[3] // hd
    rollouts = lax.axis_size("rollout")
    head_devices = lax.axis_size("head")
    devices = rollouts * head_devices
    rows = prefix_kv.shape[1]
    prefix = devices * rows
    scaling = 1.0 / math.sqrt(hd)
    c = scaling * LOG2E
    q = queries.reshape(n, heads * hd)
    g = grad_out.reshape(n, heads * hd)
    k_own = own_keys.reshape(n, hd)
    v_own = own_values.reshape(n, hd)

    vmem = pl.BlockSpec(memory_space=pltpu.VMEM)
    stat = jax.ShapeDtypeStruct((heads, n), F32)

    outgoing = jnp.broadcast_to(prefix_kv[None], (rollouts,) + prefix_kv.shape)
    outgoing = outgoing.reshape(rollouts, 2, rows, head_devices, hd).transpose(0, 3, 1, 2, 4)
    outgoing = outgoing.reshape(devices, 2, rows, hd)
    kv = lax.all_to_all(outgoing, ("rollout", "head"), 0, 0, tiled=True)

    stacked = jax.ShapeDtypeStruct((heads * n, hd), BF16)
    m_own, l_own, d_own, q_rows, g_rows = pl.pallas_call(
        functools.partial(own_stats_kernel, heads=heads, hd=hd, c=c),
        out_shape=(stat, stat, stat, stacked, stacked),
        in_specs=[vmem] * 5,
        out_specs=(vmem,) * 5,
        compiler_params=pltpu.CompilerParams(vmem_limit_bytes=12 * MIB),
        cost_estimate=pl.CostEstimate(
            flops=4 * heads * n * n * hd, bytes_accessed=3 << 20, transcendentals=heads * n * n
        ),
        name="own_stats",
    )(lengths.reshape(1, 1), q, g, k_own, v_own)

    grads, shift, row_dot = pl.pallas_call(
        functools.partial(prefix_kernel, heads=heads, hd=hd, c=c, scaling=scaling),
        out_shape=(jax.ShapeDtypeStruct((devices, 2, rows, hd), BF16), stat, stat),
        in_specs=[vmem] * 6,
        out_specs=(vmem, vmem, vmem),
        scratch_shapes=[
            pltpu.VMEM((prefix, heads * n), F32),
            pltpu.VMEM((prefix, heads * n), F32),
            pltpu.VMEM((prefix, heads * n), BF16),
            pltpu.VMEM((prefix, heads * n), BF16),
            pltpu.VMEM((heads, n), F32),
            pltpu.VMEM((heads, n), F32),
        ],
        compiler_params=pltpu.CompilerParams(vmem_limit_bytes=28 * MIB),
        cost_estimate=pl.CostEstimate(
            flops=8 * heads * n * prefix * hd, bytes_accessed=3 << 20, transcendentals=heads * n * prefix
        ),
        name="prefix_grads",
    )(q_rows, g_rows, kv, m_own, l_own, d_own)

    parts = lax.all_to_all(grads, ("rollout", "head"), 0, 0, tiled=True)

    dq, own = pl.pallas_call(
        functools.partial(rest_kernel, heads=heads, hd=hd, c=c, scaling=scaling),
        out_shape=(
            jax.ShapeDtypeStruct((n, heads * hd), BF16),
            jax.ShapeDtypeStruct((2, n, hd), BF16),
        ),
        in_specs=[vmem] * 7,
        out_specs=(vmem, vmem),
        scratch_shapes=[
            pltpu.VMEM((hd, prefix + n), BF16),
            pltpu.VMEM((n, heads * n), BF16),
            pltpu.VMEM((prefix + n, n), BF16),
        ],
        compiler_params=pltpu.CompilerParams(vmem_limit_bytes=24 * MIB),
        cost_estimate=pl.CostEstimate(
            flops=8 * heads * n * (prefix + n) * hd,
            bytes_accessed=4 << 20,
            transcendentals=heads * n * (prefix + n),
        ),
        name="query_and_own_grads",
    )(q_rows, g_rows, kv, k_own, v_own, shift, row_dot)

    grad_prefix = pl.pallas_call(
        sum_kernel,
        out_shape=jax.ShapeDtypeStruct((2, rows, head_devices * hd), BF16),
        in_specs=[vmem],
        out_specs=vmem,
        compiler_params=pltpu.CompilerParams(vmem_limit_bytes=4 * MIB),
        name="sum_rollouts",
    )(parts.reshape(rollouts, head_devices, 2, rows, hd))

    return (
        dq.reshape(1, n, 1, heads * hd),
        own.reshape(2, 1, n, 1, hd),
        grad_prefix,
    )


def solution(mesh):
    placed = (
        P(("prompt", "rollout"), None, "head", None),
        P(("prompt", "rollout"), None, "head", None),
        P(("prompt", "rollout"), None, "head", None),
        P(("prompt", "rollout"), None, "head", None),
        P(None, ("prompt", "rollout", "head"), None),
        P(("prompt", "rollout")),
    )
    return jax.shard_map(
        per_device,
        mesh=mesh,
        in_specs=placed,
        out_specs=(
            P(("prompt", "rollout"), None, "head", None),
            P(None, ("prompt", "rollout"), None, "head", None),
            P(None, ("prompt", "rollout", "head"), None),
        ),
        check_vma=False,
    )
```

```python
import functools
import math

import jax
import jax.numpy as jnp
from jax import lax
from jax.experimental import pallas as pl
from jax.experimental.pallas import tpu as pltpu
from jax.sharding import PartitionSpec as P

F32 = jnp.float32
BF16 = jnp.bfloat16
NEG = -1e30
LOG2E = math.log2(math.e)
MIB = 1024 * 1024


def dot_last(a, b):
    return lax.dot_general(a, b, (((1,), (1,)), ((), ())), preferred_element_type=F32)


def dot_plain(a, b):
    return lax.dot_general(a, b, (((1,), (0,)), ((), ())), preferred_element_type=F32)


def fold(x, op):
    parts = [x[i : i + 8] for i in range(0, x.shape[0], 8)]
    while len(parts) > 1:
        parts = [
            op(parts[i], parts[i + 1]) if i + 1 < len(parts) else parts[i]
            for i in range(0, len(parts), 2)
        ]
    return parts[0]


def causal(rows_of_keys, first_key, columns, first_column):
    key = lax.broadcasted_iota(jnp.int32, (rows_of_keys, columns), 0) + first_key
    row = lax.broadcasted_iota(jnp.int32, (rows_of_keys, columns), 1) + first_column
    return key <= row


def own_stats_kernel(
    len_ref, q_ref, g_ref, k_ref, v_ref, m_ref, l_ref, d_ref, qs_ref, gs_ref, *, heads, hd, c
):
    n = q_ref.shape[0]
    half = n // 2
    live = lax.broadcasted_iota(jnp.int32, (n, hd), 0) < len_ref[...]
    for h in range(heads):
        q = q_ref[:, h * hd : (h + 1) * hd]
        g = g_ref[:, h * hd : (h + 1) * hd]
        g = jnp.where(live, g, jnp.zeros_like(g))
        qs_ref[h * n : (h + 1) * n] = q
        gs_ref[h * n : (h + 1) * n] = g
        for b in range(2):
            cols = slice(b * half, (b + 1) * half)
            keys = (b + 1) * half
            s = dot_last(k_ref[0:keys], q[cols]) * c
            s = jnp.where(causal(keys, 0, half, b * half), s, NEG)
            m = jnp.max(fold(s, jnp.maximum), axis=0, keepdims=True)
            p = jnp.exp2(s - m)
            dp = dot_last(v_ref[0:keys], g[cols])
            m_ref[h : h + 1, cols] = m
            l_ref[h : h + 1, cols] = jnp.sum(fold(p, jnp.add), axis=0, keepdims=True)
            d_ref[h : h + 1, cols] = jnp.sum(fold(p * dp, jnp.add), axis=0, keepdims=True)


def prefix_kernel(
    qs_ref, gs_ref, kv_ref, m_ref, l_ref, d_ref,
    send_ref, shift_ref, dot_ref,
    p_ref, dp_ref, w_ref, ds_ref, inv_ref, total_ref,
    *, heads, hd, c, scaling
):
    n = qs_ref.shape[0] // heads
    devices, _, rows, _ = kv_ref.shape
    prefix = devices * rows
    step, width, last = 256, 256, 1024
    chunks = prefix // step
    tiles = []
    for t in range(heads * n // width):
        h = t * width // n
        first = t * width - h * n
        tiles.append((slice(h, h + 1), slice(first, first + width), slice(t * width, (t + 1) * width)))

    def block(index, which):
        per = step // rows
        return kv_ref[index * per : (index + 1) * per, which].reshape(step, hd)

    def weigh(exact):
        for head, cols, at in tiles:
            q = qs_ref[at]
            g = gs_ref[at]
            m = m_ref[head, cols]
            l = l_ref[head, cols]
            d = d_ref[head, cols]
            if exact:
                own = m
                for i in range(chunks):
                    top = fold(dot_last(block(i, 0), q) * c, jnp.maximum)
                    m = jnp.maximum(m, jnp.max(top, axis=0, keepdims=True))
                again = jnp.exp2(own - m)
                l = l * again
                d = d * again
            l8 = jnp.zeros((8, width), F32)
            d8 = jnp.zeros((8, width), F32)
            for i in range(chunks):
                part = slice(i * step, (i + 1) * step)
                p = jnp.exp2(dot_last(block(i, 0), q) * c - m)
                l8 = l8 + fold(p, jnp.add)
                p_ref[part, at] = p
            for i in range(chunks):
                part = slice(i * step, (i + 1) * step)
                dp = dot_last(block(i, 1), g)
                d8 = d8 + fold(p_ref[part, at] * dp, jnp.add)
                dp_ref[part, at] = dp
            l = l + jnp.sum(l8, axis=0, keepdims=True)
            d = d + jnp.sum(d8, axis=0, keepdims=True)
            inv = 1.0 / l
            total_ref[head, cols] = l
            inv_ref[head, cols] = inv
            shift_ref[head, cols] = m + jnp.log2(l)
            dot_ref[head, cols] = d * inv

    weigh(False)
    fits = jnp.max(total_ref[...]) < 2.0**60

    @pl.when(jnp.logical_not(fits))
    def _():
        weigh(True)

    for e in range(prefix // last):
        for head, cols, at in tiles:
            inv = inv_ref[head, cols]
            for i in range(last // step):
                part = slice(e * last + i * step, e * last + (i + 1) * step)
                w_ref[part, at] = (p_ref[part, at] * inv).astype(BF16)
        part = slice(e * last, (e + 1) * last)
        owners = slice(e * last // rows, (e + 1) * last // rows)
        shape = (last // rows, rows, hd)
        grad_v = dot_plain(w_ref[part], gs_ref[...])
        send_ref[owners, 1] = grad_v.astype(BF16).reshape(shape)
    for e in range(prefix // last):
        for head, cols, at in tiles:
            inv = inv_ref[head, cols]
            d = dot_ref[head, cols]
            for i in range(last // step):
                part = slice(e * last + i * step, e * last + (i + 1) * step)
                ds_ref[part, at] = (p_ref[part, at] * inv * (dp_ref[part, at] - d)).astype(BF16)
        part = slice(e * last, (e + 1) * last)
        owners = slice(e * last // rows, (e + 1) * last // rows)
        grad_k = dot_plain(ds_ref[part], qs_ref[...]) * scaling
        send_ref[owners, 0] = grad_k.astype(BF16).reshape(shape)


def rest_kernel(
    qs_ref, gs_ref, kv_ref, k_ref, v_ref, shift_ref, dot_ref,
    dq_ref, own_ref,
    kt_ref, w_ref, ds_ref,
    *, heads, hd, c, scaling
):
    n = qs_ref.shape[0] // heads
    devices, _, rows, _ = kv_ref.shape
    prefix = devices * rows
    step = 256
    per = step // rows
    half = n // 2
    chunks = prefix // step
    for i in range(chunks):
        k = kv_ref[i * per : (i + 1) * per, 0].reshape(step, hd)
        kt_ref[:, i * step : (i + 1) * step] = k.T
    kt_ref[:, prefix:] = k_ref[...].T
    for h in range(heads):
        shift = shift_ref[h : h + 1]
        d = dot_ref[h : h + 1]
        q = qs_ref[h * n : (h + 1) * n]
        g = gs_ref[h * n : (h + 1) * n]
        for i in range(chunks):
            k = kv_ref[i * per : (i + 1) * per, 0].reshape(step, hd)
            v = kv_ref[i * per : (i + 1) * per, 1].reshape(step, hd)
            w = jnp.exp2(dot_last(k, q) * c - shift)
            ds_ref[i * step : (i + 1) * step] = (w * (dot_last(v, g) - d)).astype(BF16)
        for b in range(2):
            cols = slice(b * half, (b + 1) * half)
            keys = (b + 1) * half
            s = dot_last(k_ref[0:keys], q[cols]) * c
            s = jnp.where(causal(keys, 0, half, b * half), s, NEG)
            w = jnp.exp2(s - shift[:, cols])
            ds = (w * (dot_last(v_ref[0:keys], g[cols]) - d[:, cols])).astype(BF16)
            at = slice(h * n + b * half, h * n + (b + 1) * half)
            w_ref[0:keys, at] = w.astype(BF16)
            ds_ref[prefix : prefix + keys, cols] = ds
            if keys < n:
                empty = jnp.zeros((n - keys, half), BF16)
                w_ref[keys:, at] = empty
                ds_ref[prefix + keys :, cols] = empty
        dqt = dot_plain(kt_ref[...], ds_ref[...]) * scaling
        dq_ref[:, h * hd : (h + 1) * hd] = dqt.T.astype(BF16)
        own = dot_plain(ds_ref[prefix:], q)
        total = own if h == 0 else total + own
    own_ref[0] = (total * scaling).astype(BF16)
    own_ref[1] = dot_plain(w_ref[...], gs_ref[...]).astype(BF16)


def sum_kernel(x_ref, out_ref):
    groups, heads, _, rows, hd = x_ref.shape
    for h in range(heads):
        total = x_ref[0, h].astype(F32)
        for r in range(1, groups):
            total = total + x_ref[r, h].astype(F32)
        out_ref[:, :, h * hd : (h + 1) * hd] = total.astype(BF16)


def per_device(queries, own_keys, own_values, grad_out, prefix_kv, lengths):
    hd = own_keys.shape[3]
    n = queries.shape[1]
    heads = queries.shape[3] // hd
    rollouts = lax.axis_size("rollout")
    head_devices = lax.axis_size("head")
    devices = rollouts * head_devices
    rows = prefix_kv.shape[1]
    prefix = devices * rows
    scaling = 1.0 / math.sqrt(hd)
    c = scaling * LOG2E
    q = queries.reshape(n, heads * hd)
    g = grad_out.reshape(n, heads * hd)
    k_own = own_keys.reshape(n, hd)
    v_own = own_values.reshape(n, hd)

    vmem = pl.BlockSpec(memory_space=pltpu.VMEM)
    stat = jax.ShapeDtypeStruct((heads, n), F32)

    outgoing = jnp.broadcast_to(prefix_kv[None], (rollouts,) + prefix_kv.shape)
    outgoing = outgoing.reshape(rollouts, 2, rows, head_devices, hd).transpose(0, 3, 1, 2, 4)
    outgoing = outgoing.reshape(devices, 2, rows, hd)
    kv = lax.all_to_all(outgoing, ("rollout", "head"), 0, 0, tiled=True)

    stacked = jax.ShapeDtypeStruct((heads * n, hd), BF16)
    m_own, l_own, d_own, q_rows, g_rows = pl.pallas_call(
        functools.partial(own_stats_kernel, heads=heads, hd=hd, c=c),
        out_shape=(stat, stat, stat, stacked, stacked),
        in_specs=[vmem] * 5,
        out_specs=(vmem,) * 5,
        compiler_params=pltpu.CompilerParams(vmem_limit_bytes=12 * MIB),
        cost_estimate=pl.CostEstimate(
            flops=4 * heads * n * n * hd, bytes_accessed=3 << 20, transcendentals=heads * n * n
        ),
        name="own_stats",
    )(lengths.reshape(1, 1), q, g, k_own, v_own)

    grads, shift, row_dot = pl.pallas_call(
        functools.partial(prefix_kernel, heads=heads, hd=hd, c=c, scaling=scaling),
        out_shape=(jax.ShapeDtypeStruct((devices, 2, rows, hd), BF16), stat, stat),
        in_specs=[vmem] * 6,
        out_specs=(vmem, vmem, vmem),
        scratch_shapes=[
            pltpu.VMEM((prefix, heads * n), F32),
            pltpu.VMEM((prefix, heads * n), F32),
            pltpu.VMEM((prefix, heads * n), BF16),
            pltpu.VMEM((prefix, heads * n), BF16),
            pltpu.VMEM((heads, n), F32),
            pltpu.VMEM((heads, n), F32),
        ],
        compiler_params=pltpu.CompilerParams(vmem_limit_bytes=28 * MIB),
        cost_estimate=pl.CostEstimate(
            flops=8 * heads * n * prefix * hd, bytes_accessed=3 << 20, transcendentals=heads * n * prefix
        ),
        name="prefix_grads",
    )(q_rows, g_rows, kv, m_own, l_own, d_own)

    parts = lax.all_to_all(grads, ("rollout", "head"), 0, 0, tiled=True)

    dq, own = pl.pallas_call(
        functools.partial(rest_kernel, heads=heads, hd=hd, c=c, scaling=scaling),
        out_shape=(
            jax.ShapeDtypeStruct((n, heads * hd), BF16),
            jax.ShapeDtypeStruct((2, n, hd), BF16),
        ),
        in_specs=[vmem] * 7,
        out_specs=(vmem, vmem),
        scratch_shapes=[
            pltpu.VMEM((hd, prefix + n), BF16),
            pltpu.VMEM((n, heads * n), BF16),
            pltpu.VMEM((prefix + n, n), BF16),
        ],
        compiler_params=pltpu.CompilerParams(vmem_limit_bytes=24 * MIB),
        cost_estimate=pl.CostEstimate(
            flops=8 * heads * n * (prefix + n) * hd,
            bytes_accessed=4 << 20,
            transcendentals=heads * n * (prefix + n),
        ),
        name="query_and_own_grads",
    )(q_rows, g_rows, kv, k_own, v_own, shift, row_dot)

    grad_prefix = pl.pallas_call(
        sum_kernel,
        out_shape=jax.ShapeDtypeStruct((2, rows, head_devices * hd), BF16),
        in_specs=[vmem],
        out_specs=vmem,
        compiler_params=pltpu.CompilerParams(vmem_limit_bytes=4 * MIB),
        name="sum_rollouts",
    )(parts.reshape(rollouts, head_devices, 2, rows, hd))

    return (
        dq.reshape(1, n, 1, heads * hd),
        own.reshape(2, 1, n, 1, hd),
        grad_prefix,
    )


def solution(mesh):
    placed = (
        P(("prompt", "rollout"), None, "head", None),
        P(("prompt", "rollout"), None, "head", None),
        P(("prompt", "rollout"), None, "head", None),
        P(("prompt", "rollout"), None, "head", None),
        P(None, ("prompt", "rollout", "head"), None),
        P(("prompt", "rollout")),
    )
    return jax.shard_map(
        per_device,
        mesh=mesh,
        in_specs=placed,
        out_specs=(
            P(("prompt", "rollout"), None, "head", None),
            P(None, ("prompt", "rollout"), None, "head", None),
            P(None, ("prompt", "rollout", "head"), None),
        ),
        check_vma=False,
    )
```
